32 devices in a mesh: groups: 2 (over x), row: 4 (over y, core), col: 4 (over z).
Axes of the slice: x: 2, y: 2, z: 4, core: 2. Of those that a mesh axis runs over, the one named last changes fastest.
Arguments:
- noise_field: float32 [3, 2, 4096], P(None, None, ('groups', 'row', 'col')), parts along dimension 2, may hold values from -6 to 6
- offsets: int32 [3, 4096], P(None, ('groups', 'row', 'col')), parts along dimension 1, may hold values from 0 to 7
- tile_list: int32 [8, 4, 2, 2], P(('groups', 'row'), 'col'), parts along dimension 0, may hold values from -1 to 3, as said below
- send_cells: int32 [8, 4, 16, 16], P(('groups', 'row'), 'col'), parts along dimension 0, may hold values from 0 to 131071, as said below
- bead_slot: int32 [4096], P(('groups', 'row', 'col')), parts along dimension 0, may hold values from 0 to 255, as said below
- spectral: float32 [2, 3, 2, 256, 128, 128], P(None, None, None, ('groups', 'row'), 'col'), parts along dimension 3, may hold values from -6 to 6
Outputs:
- velocity: float32 [3, 2, 4096], P(None, None, ('groups', 'row', 'col')), parts along dimension 2
The draws below stay inside these ranges and needn't reach their ends.
There are 2 independent parts, one for each index of `groups`. The reference program is written for one: setup_inputs(seed, part) draws one part's arguments, and reference() takes and returns one part's arrays. A program takes and returns all parts, laid end to end along the dimension named above; each array names one. Nothing has to cross between parts.
Inputs may be any that keep to these rules, and one draw needn't show every extreme that they name: `tile_list`: for each device the first slots name distinct (row tile, column tile) pairs with row tile below 4 and column tile below 4; the remaining slots hold -1 in both entries. Some device uses all 2 slots, some device fewer. `send_cells`: entries are local cell indices of the holder's block of 128 x 32 x 32 cells, first dimension slowest. `bead_slot`: within one owner's 128 beads no value repeats, so a holder serves one owner through at most 16 slots; every owner takes all 16 slots of one holder.
All inputs are finite; a program needn't handle non-finite values.
Results may differ from the reference program's by a relative error of at most 0.0039.
Values may be sent and summed in bfloat16 or wider, within the bound.
No kernel may reach another device: no remote copies, remote signals or barrier semaphores. Data moves between devices by JAX's collectives and lax.ppermute only.
A program may use at most 128 MiB of HBM per device.

```python
import math
import jax
import jax.numpy as jnp
from jax import lax

MONOMER_PER_UNIT = 128
NVEC = 2
TB = 128
G = 128
PERIOD = 8
SHARING_UNITS = 16
NB = 2048
RT = 4
CT = 4
SLOTS = 2
CAP = 16
YSLAB = 32
ZSLAB = 32
N_ROW = 4
N_COL = 4


def draw_tile_list(key, part):
    divided_seeds = jax.random.split(jax.random.fold_in(key, 11), 4)
    device_ids = jnp.arange(SHARING_UNITS, dtype=jnp.int32)
    message_batches = jax.random.randint(divided_seeds[0], (SHARING_UNITS,), 0, 8)
    coarsest_tier = jax.random.randint(divided_seeds[1], (SHARING_UNITS,), 1, 4)
    tier_sequence = jnp.where(message_batches == 0, 8, coarsest_tier)
    full_device = jax.random.randint(divided_seeds[2], (), 0, SHARING_UNITS)
    tier_sequence = jnp.where(device_ids == full_device, 8, tier_sequence)
    tier_sequence = jnp.where(device_ids == (full_device + 1) % SHARING_UNITS, 1, tier_sequence)
    counts = jnp.maximum(1, SLOTS * tier_sequence // 8)
    pair_ids = jnp.arange(RT * CT, dtype=jnp.int32)
    slot_ids = jnp.arange(SLOTS, dtype=jnp.int32)

    def per_device(subkey, device, limit):
        scores = jax.random.permutation(subkey, RT * CT)
        scores = jnp.where((device == full_device) & (pair_ids == RT * CT - 1), -1, scores)
        ranked = jnp.argsort(scores)[:SLOTS]
        active = slot_ids < limit
        return jnp.stack([jnp.where(active, ranked // CT, -1), jnp.where(active, ranked % CT, -1)])
    final_output = jax.vmap(per_device)(jax.random.split(divided_seeds[3], SHARING_UNITS), device_ids, counts)
    return final_output.reshape(N_ROW, N_COL, 2, SLOTS).astype(jnp.int32)


def draw_send_cells(key, part):
    cell_count = G * YSLAB * ZSLAB
    values = jax.random.randint(jax.random.fold_in(key, 23), (N_ROW, N_COL, CAP, SHARING_UNITS), 0, cell_count)
    position = jnp.arange(N_ROW * N_COL * CAP * SHARING_UNITS, dtype=jnp.int32).reshape(N_ROW, N_COL, CAP, SHARING_UNITS)
    values = jnp.where(position == 0, cell_count - 1, jnp.where(position == 1, 0, values))
    return values.astype(jnp.int32)


def draw_bead_slot(key, part):
    divided_seeds = jax.random.split(jax.random.fold_in(key, 37), 2)
    rotate = jax.random.randint(divided_seeds[0], (), 0, SHARING_UNITS)
    owners = jnp.arange(SHARING_UNITS, dtype=jnp.int32)
    full_holder = (owners + rotate) % SHARING_UNITS
    code_ids = jnp.arange(SHARING_UNITS * CAP, dtype=jnp.int32)

    def by_holding_unit(subkey, holder):
        scores = jax.random.permutation(subkey, SHARING_UNITS * CAP)
        scores = jnp.where(code_ids % SHARING_UNITS == holder, code_ids // SHARING_UNITS - CAP, scores)
        return jnp.argsort(scores)[:MONOMER_PER_UNIT]
    final_output = jax.vmap(by_holding_unit)(jax.random.split(divided_seeds[1], SHARING_UNITS), full_holder)
    return final_output.reshape(-1).astype(jnp.int32)


def place_ends(result, stream_key, smallest, high):
    dims = result.shape
    place = [jax.random.randint(jax.random.fold_in(stream_key, axis), (), 0, dims[axis]) for axis in range(len(dims))]
    result = result.at[tuple(place)].set(smallest)
    longest = dims.index(max(dims))
    place[longest] = (place[longest] + 1) % dims[longest]
    return result.at[tuple(place)].set(high)


def block_levels(stream_key, dims, cuts, smallest, high):
    gain = 1.0
    for axis_at, shards_of in cuts:
        steps = jax.random.uniform(jax.random.fold_in(jax.random.fold_in(stream_key, 6), axis_at), (shards_of,), jnp.float32, smallest / len(cuts), high / len(cuts))
        gain = gain * jnp.repeat(jnp.exp(steps), dims[axis_at] // shards_of).reshape((-1,) + (1,) * (len(dims) - 1 - axis_at))
    return gain


def centred(rng, dims, scale, most, shards=(), kind=jnp.bfloat16):
    values = scale * jax.random.normal(rng, dims, jnp.float32)
    if shards:
        values = values * block_levels(rng, dims, shards, -0.22, 0.18)
    return jnp.clip(values, -most, most).astype(kind)


def setup_inputs(seed: int = 0, part: int = 0) -> dict:
    arg_keys = jax.random.split(jax.random.key(seed), 7)
    part_splits = jax.random.split(jax.random.fold_in(arg_keys[6], part), 7)
    noise_field = centred(part_splits[0], (3, NVEC, NB), 1.0, 6.0, ((2, 16),), jnp.float32)
    offsets = place_ends(jax.random.randint(part_splits[1], (3, NB), 0, PERIOD), jax.random.fold_in(part_splits[1], 1), 0, PERIOD - 1).astype(jnp.int32)
    tile_list = draw_tile_list(jax.random.fold_in(jax.random.fold_in(arg_keys[6], part), 71), part)
    send_cells = draw_send_cells(jax.random.fold_in(jax.random.fold_in(arg_keys[6], part), 71), part)
    bead_slot = draw_bead_slot(jax.random.fold_in(jax.random.fold_in(arg_keys[6], part), 71), part)
    spectral = centred(part_splits[5], (2, 3, NVEC, G, G, G), 1.0, 6.0, ((3, 4), (4, 4)), jnp.float32)
    return dict(noise_field=noise_field, offsets=offsets, tile_list=tile_list, send_cells=send_cells, bead_slot=bead_slot, spectral=spectral)


cheb_coef = (1.0, 0.45, -0.2, 0.12, -0.08)
kernel_range = 1.5

def kernel_parts(displace):
    squares = displace[0] * displace[0] + displace[1] * displace[1] + displace[2] * displace[2]
    scale_sq = kernel_range * kernel_range
    envelope = jnp.exp(squares * (-0.5 / scale_sq)) / scale_sq
    entries = []
    for left_comp in range(3):
        for right_comp in range(3):
            element = displace[left_comp] * displace[right_comp]
            if left_comp == right_comp:
                element = element - squares / 3.0
            entries.append(envelope * element)
    return jnp.stack(entries)

def kernel_lookup():
    half_period = PERIOD // 2
    code_ids = jnp.arange(PERIOD ** 3, dtype=jnp.int32)
    shifted = jnp.stack([code_ids // (PERIOD * PERIOD), code_ids // PERIOD % PERIOD, code_ids % PERIOD])
    return kernel_parts((shifted - half_period).astype(jnp.float32)).astype(jnp.bfloat16)

def device_tiles(device, offsets, tile_list, lookup):
    row_idx = device // N_COL
    col_idx = device % N_COL
    tile_rows = tile_list[row_idx, col_idx, 0]
    tile_cols = tile_list[row_idx, col_idx, 1]
    active = tile_rows >= 0
    safe_rows = jnp.maximum(tile_rows, 0)
    safe_cols = jnp.maximum(tile_cols, 0)
    lane_ids = jnp.arange(TB, dtype=jnp.int32)
    row_beads = row_idx * N_COL * MONOMER_PER_UNIT + safe_rows[:, None] * TB + lane_ids[None, :]
    local_cols = safe_cols[:, None] * TB + lane_ids[None, :]
    col_beads = local_cols // MONOMER_PER_UNIT * N_COL * MONOMER_PER_UNIT + col_idx * MONOMER_PER_UNIT + local_cols % MONOMER_PER_UNIT
    half_period = PERIOD // 2
    shifted = (offsets[:, row_beads][:, :, :, None] - offsets[:, col_beads][:, :, None, :] + half_period) % PERIOD
    code_ids = (shifted[0] * PERIOD + shifted[1]) * PERIOD + shifted[2]
    kernel_tiles = lookup[:, code_ids].reshape(3, 3, SLOTS, TB, TB)
    selector = ((tile_rows[:, None] == jnp.arange(RT, dtype=jnp.int32)[None, :]) & active[:, None]).astype(jnp.float32)
    return (kernel_tiles, selector, col_beads)

def combine(partials):
    lead_shape = partials.shape[1:-1]
    grouped = partials.reshape((N_ROW, N_COL) + lead_shape + (N_COL * MONOMER_PER_UNIT,)).sum(axis=1)
    regrouped = jnp.moveaxis(grouped, 0, -2)
    return regrouped.reshape(lead_shape + (NB,))

def row_energy(offsets, tile_list, lookup):

    def per_device(device):
        kernel_tiles, selector, col_beads = device_tiles(device, offsets, tile_list, lookup)
        squared = lax.optimization_barrier(jnp.sum(jnp.square(kernel_tiles.astype(jnp.float32)), axis=(1, 4)))
        return jnp.einsum('asp,si->aip', squared, selector, precision=lax.Precision.HIGHEST).reshape(3, RT * TB)
    return combine(lax.map(per_device, jnp.arange(SHARING_UNITS, dtype=jnp.int32)))

def near_apply(vector, offsets, tile_list, lookup):
    rounded = vector.astype(jnp.bfloat16)

    def per_device(device):
        kernel_tiles, selector, col_beads = device_tiles(device, offsets, tile_list, lookup)
        pieces = rounded[:, :, col_beads].astype(jnp.float32)
        blocks = jnp.einsum('abspq,bksq->aksp', kernel_tiles.astype(jnp.float32), pieces, precision=lax.Precision.HIGHEST)
        return jnp.einsum('aksp,si->akip', blocks, selector, precision=lax.Precision.HIGHEST).reshape(3, NVEC, RT * TB)
    return combine(lax.map(per_device, jnp.arange(SHARING_UNITS, dtype=jnp.int32)))

def far_grid(spectral):
    wave_ids = jnp.arange(G, dtype=jnp.int32)
    signed = jnp.where(wave_ids < G // 2, wave_ids, wave_ids - G).astype(jnp.float32)
    wave_x = signed[:, None, None]
    wave_y = signed[None, :, None]
    wave_z = signed[None, None, :]
    wave_sq = wave_x * wave_x + wave_y * wave_y + wave_z * wave_z
    width_sq = (G / 8.0) ** 2
    amplitude = jnp.where(wave_sq > 0, math.sqrt(1.5) / (2.0 * math.pi * width_sq) ** 0.75 * jnp.exp(wave_sq * (-0.25 / width_sq)), 0.0)

    def project(source_field):
        along_k = wave_x * source_field[0] + wave_y * source_field[1] + wave_z * source_field[2]
        factor = along_k / jnp.maximum(wave_sq, 1.0)
        return jnp.stack([amplitude * (source_field[0] - wave_x * factor), amplitude * (source_field[1] - wave_y * factor), amplitude * (source_field[2] - wave_z * factor)])
    real_part = project(spectral[0])
    imag_part = project(spectral[1])
    inverse = jnp.fft.ifftn(real_part + 1j * imag_part, axes=(-3, -2, -1))
    return jnp.real(inverse) * G ** 3

def reference(noise_field, offsets, tile_list, send_cells, bead_slot, spectral):
    lookup = kernel_lookup()
    energy = row_energy(offsets, tile_list, lookup)
    scaling = 1.0 / jnp.sqrt(jnp.max(energy) + 1e-06)
    previous = noise_field
    current = scaling * near_apply(noise_field, offsets, tile_list, lookup)
    near_field = cheb_coef[0] * previous + cheb_coef[1] * current
    for degree in range(2, 5):
        following = 2.0 * (scaling * near_apply(current, offsets, tile_list, lookup)) - previous
        near_field = near_field + cheb_coef[degree] * following
        previous, current = (current, following)
    grid_field = far_grid(spectral)
    owner_ids = jnp.arange(NB, dtype=jnp.int32) // MONOMER_PER_UNIT
    source = bead_slot % SHARING_UNITS
    slot_idx = bead_slot // SHARING_UNITS
    src_row = source // N_COL
    src_col = source % N_COL
    cell_ids = send_cells[src_row, src_col, slot_idx, owner_ids]
    pos_x = cell_ids // (YSLAB * ZSLAB)
    pos_y = src_row * YSLAB + cell_ids // ZSLAB % YSLAB
    pos_z = src_col * ZSLAB + cell_ids % ZSLAB
    far_field = grid_field[:, :, pos_x, pos_y, pos_z]
    return near_field + far_field
```

```python
import functools
import math

import jax
import jax.numpy as jnp
import ml_dtypes
import numpy as np
from jax import lax
from jax.experimental import pallas as pl
from jax.experimental.pallas import tpu as pltpu
from jax.sharding import PartitionSpec as P

TB = 128
PERIOD = 8
SITES = PERIOD**3
HEAD = 16
CODE, SLOT, ROW_TILE, COL_TILE = 6, 7, 8, 9
UNIT_AXES = ("row", "col")
VMEM_BYTES = 56 * 1024 * 1024

cheb_coef = (1.0, 0.45, -0.2, 0.12, -0.08)
kernel_range = 1.5

F32 = jnp.float32
BF16 = jnp.bfloat16


def kernel_tables():
    ids = np.arange(SITES)
    coords = np.stack([ids // PERIOD**2, ids // PERIOD % PERIOD, ids % PERIOD])
    half = PERIOD // 2
    displace = (coords[:, :, None] - coords[:, None, :] + half) % PERIOD - half
    displace = displace.astype(np.float32)
    squares = (displace * displace).sum(0)
    scale_sq = np.float32(kernel_range * kernel_range)
    envelope = np.exp(squares * np.float32(-0.5 / scale_sq)) / scale_sq
    table = np.zeros((3, SITES, 3, SITES), np.float32)
    for left in range(3):
        for right in range(3):
            element = displace[left] * displace[right]
            if left == right:
                element = element - squares / np.float32(3.0)
            table[left, :, right, :] = envelope * element
    table = table.astype(ml_dtypes.bfloat16)
    squared = np.square(table.astype(np.float32)).sum(2)
    high = squared.astype(ml_dtypes.bfloat16)
    low = (squared - high.astype(np.float32)).astype(ml_dtypes.bfloat16)
    energy = np.concatenate([high, low], axis=2)
    return table.reshape(3 * SITES, 3 * SITES), energy.reshape(3 * SITES, 2 * SITES)


def wave_tables(length):
    ids = np.arange(length)
    angles = (ids[:, None] * ids[None, :] % length) * (2.0 * math.pi / length)
    return np.stack([np.cos(angles), np.sin(angles)]).astype(np.float32)


def last_transform(length):
    cos, sin = wave_tables(length)
    whole = np.concatenate(
        [np.concatenate([cos, -sin], axis=1), np.concatenate([-sin, -cos], axis=1)], axis=0
    )
    return whole.astype(ml_dtypes.bfloat16)


def split(value):
    high = value.astype(BF16)
    return high, (value - high.astype(F32)).astype(BF16)


def quotient(value, by):
    if by & (by - 1) == 0:
        return lax.shift_right_logical(value, int(math.log2(by)))
    return value // by


def remainder(value, by):
    if by & (by - 1) == 0:
        return value & (by - 1)
    return value % by


def dot_nt(left, right):
    return lax.dot_general(left, right, (((1,), (1,)), ((), ())), preferred_element_type=F32)


def dot_tn(left, right):
    return lax.dot_general(left, right, (((0,), (0,)), ((), ())), preferred_element_type=F32)


def dot(left, right):
    return jnp.dot(left, right, preferred_element_type=F32)


def lanes_from(value, start, width):
    if start % 128 == 0:
        padded = -(-width // 128) * 128
        return value[:, start : start + padded]
    total = value.shape[1]
    return pltpu.roll(value, total - start, 1)[:, : -(-width // 128) * 128]


def pack_kernel(cols, ids_ref, tiles_ref, noise_ref, offsets_ref, cells_ref, slot_ref, out_ref):
    units = out_ref.shape[0]
    slots = tiles_ref.shape[3]
    code = (offsets_ref[0:1, :] * PERIOD + offsets_ref[1:2, :]) * PERIOD + offsets_ref[2:3, :]
    lane = lax.broadcasted_iota(jnp.int32, (1, TB), 1)
    row_tile = jnp.full((1, TB), -1, jnp.int32)
    col_tile = jnp.full((1, TB), -1, jnp.int32)
    for slot in range(slots):
        tile_row = tiles_ref[0, 0, 0, slot]
        tile_col = tiles_ref[0, 0, 1, slot]
        active = tile_row >= 0
        row_unit = jnp.where(active, ids_ref[0] * cols + tile_row, -1)
        col_unit = jnp.where(active, tile_col * cols + ids_ref[1], -1)
        row_tile = jnp.where(lane == slot, row_unit, row_tile)
        col_tile = jnp.where(lane == slot, col_unit, col_tile)
    noise = jnp.concatenate([noise_ref[0], noise_ref[1], noise_ref[2]], axis=0)
    head = jnp.concatenate([code, slot_ref[...], row_tile, col_tile], axis=0).astype(F32)
    cells = cells_ref[0, 0].astype(F32)
    caps, peers = cells.shape
    out_ref[0] = jnp.zeros(out_ref.shape[1:], F32)
    out_ref[0, 0:6, :] = noise
    out_ref[0, 6:10, :] = head
    out_ref[0, HEAD : HEAD + caps, 0:peers] = cells
    block = out_ref[0]
    for unit in range(1, units):
        out_ref[unit] = block


def pack(ids, noise_field, offsets, tile_list, send_cells, bead_slot, units, cols):
    caps = send_cells.shape[2]
    rows = HEAD + -(-caps // 8) * 8
    vmem = pl.BlockSpec(memory_space=pltpu.VMEM)
    smem = pl.BlockSpec(memory_space=pltpu.SMEM)
    return pl.pallas_call(
        functools.partial(pack_kernel, cols),
        out_shape=jax.ShapeDtypeStruct((units, rows, TB), F32),
        in_specs=[smem, smem, vmem, vmem, vmem, vmem],
        out_specs=vmem,
        name="pack_inputs",
    )(ids, tile_list, noise_field, offsets, send_cells, bead_slot.reshape(1, TB))


def signed(ids, length):
    return jnp.where(ids < length // 2, ids, ids - length).astype(F32)


def spectrum_kernel(rows_x, ids_ref, spec_ref, turn_ref, out_ref):
    _, comps, vecs, part_x, rows_y, length = spec_ref.shape
    shape = (part_x, rows_y, length)
    first_x = ids_ref[0] * rows_x + pl.program_id(0) * part_x
    first_y = ids_ref[1] * rows_y
    wave = (
        signed(first_x + lax.broadcasted_iota(jnp.int32, shape, 0), length),
        signed(first_y + lax.broadcasted_iota(jnp.int32, shape, 1), length),
        signed(lax.broadcasted_iota(jnp.int32, shape, 2), length),
    )
    wave_sq = wave[0] * wave[0] + wave[1] * wave[1] + wave[2] * wave[2]
    width_sq = (length / 8.0) ** 2
    amplitude = jnp.where(
        wave_sq > 0,
        math.sqrt(1.5) / (2.0 * math.pi * width_sq) ** 0.75 * jnp.exp(wave_sq * (-0.25 / width_sq)),
        0.0,
    )
    damped = amplitude / jnp.maximum(wave_sq, 1.0)
    for vec in range(vecs):
        hat = []
        for part in range(2):
            source = [spec_ref[part, comp, vec] for comp in range(comps)]
            along = wave[0] * source[0] + wave[1] * source[1] + wave[2] * source[2]
            factor = along * damped
            hat.append(
                [
                    (amplitude * source[comp] - wave[comp] * factor)
                    .astype(BF16)
                    .reshape(part_x * rows_y, length)
                    for comp in range(comps)
                ]
            )
        for comp in range(comps):
            both = jnp.concatenate([hat[0][comp], hat[1][comp]], axis=1)
            turned = dot_nt(turn_ref[...], both).astype(BF16)
            at = (comp * vecs + vec) * length
            out_ref[0, at : at + length, :] = turned[:length]
            out_ref[1, at : at + length, :] = turned[length:]


def spectrum(ids, spectral):
    _, comps, vecs, rows_x, rows_y, length = spectral.shape
    part_x = max(1, min(rows_x, 256 // rows_y))
    while rows_x % part_x:
        part_x -= 1
    steps = rows_x // part_x
    fields = comps * vecs * length
    return pl.pallas_call(
        functools.partial(spectrum_kernel, rows_x),
        grid=(steps,),
        out_shape=jax.ShapeDtypeStruct((2, fields, rows_x * rows_y), BF16),
        in_specs=[
            pl.BlockSpec(memory_space=pltpu.SMEM),
            pl.BlockSpec((2, comps, vecs, part_x, rows_y, length), lambda i: (0, 0, 0, i, 0, 0)),
            pl.BlockSpec((2 * length, 2 * length), lambda i: (0, 0)),
        ],
        out_specs=pl.BlockSpec((2, fields, part_x * rows_y), lambda i: (0, 0, i)),
        compiler_params=pltpu.CompilerParams(vmem_limit_bytes=VMEM_BYTES),
        cost_estimate=pl.CostEstimate(
            flops=2 * 2 * fields * rows_x * rows_y * 2 * length,
            bytes_accessed=spectral.size * 4 + 4 * fields * rows_x * rows_y,
            transcendentals=rows_x * rows_y * length,
        ),
        name="spectrum",
    )(ids, spectral, jnp.asarray(last_transform(length)))


def find_cells(cols, slab_y, slab_z, packed_ref, place_ref):
    units = packed_ref.shape[0]
    caps = packed_ref.shape[1] - HEAD
    entries = units * caps
    cells = packed_ref[:, HEAD:, :].reshape(entries, TB)
    cells = jnp.transpose(cells).astype(jnp.int32)
    owners = -(-units // 16) * 16
    cells = cells[:owners]
    entry = lax.broadcasted_iota(jnp.int32, cells.shape, 1)
    holder = quotient(entry, caps)
    holder_row = quotient(holder, cols)
    holder_col = holder - holder_row * cols
    rest = quotient(cells, slab_z)
    digits = [
        quotient(rest, slab_y),
        holder_row * slab_y + remainder(rest, slab_y),
        holder_col * slab_z + remainder(cells, slab_z),
    ]
    digits = jnp.concatenate([d.astype(F32).astype(BF16) for d in digits], axis=0)
    which = lax.broadcasted_iota(jnp.int32, (entries, TB), 0)
    unit_ids = lax.broadcasted_iota(jnp.int32, (owners, TB), 0)

    def one_unit(unit, carry):
        slot = packed_ref[unit, SLOT : SLOT + 1, :].astype(jnp.int32)
        index = remainder(slot, units) * caps + quotient(slot, units)
        chosen = jnp.where(which == index, 1.0, 0.0).astype(BF16)
        found = dot(digits, chosen)
        for digit in range(3):
            rows = found[digit * owners : (digit + 1) * owners]
            place_ref[unit, digit : digit + 1, :] = jnp.sum(
                jnp.where(unit_ids == unit, rows, 0.0), axis=0, keepdims=True
            )
        return carry

    lax.fori_loop(0, units, one_unit, 0, unroll=units <= 16)


def sample_kernel(
    cols, slabs, rows, ids_ref, packed_ref, field_ref, wave_ref, out_ref, place_ref, phase_ref
):
    length = wave_ref.shape[1]
    group = out_ref.shape[0]
    fields = field_ref.shape[1] // length
    step = pl.program_id(0)

    @pl.when(step == 0)
    def _():
        find_cells(cols, slabs[0], slabs[1], packed_ref, place_ref)

    beads = group * TB
    place = [
        jnp.concatenate(
            [place_ref[step * group + unit, axis : axis + 1, :] for unit in range(group)], axis=1
        ).astype(jnp.int32)
        for axis in range(3)
    ]
    position = lax.broadcasted_iota(jnp.int32, (length, beads), 0)

    def phases(axis):
        count = rows[axis]
        first = pl.multiple_of(ids_ref[axis] * count, count)
        chosen = jnp.where(position == place[axis], 1.0, 0.0).astype(BF16)
        result = []
        for part in range(2):
            high, low = split(wave_ref[part, pl.ds(first, count), :])
            result.append(dot(high, chosen) + dot(low, chosen))
        return result

    cos_x, sin_x = phases(0)
    cos_y, sin_y = phases(1)
    rows_y = rows[1]
    for x in range(rows[0]):
        cos_one, sin_one = cos_x[x : x + 1], sin_x[x : x + 1]
        at = slice(x * rows_y, (x + 1) * rows_y)
        phase_ref[0, at, :] = (cos_one * cos_y - sin_one * sin_y).astype(BF16)
        phase_ref[1, at, :] = (cos_one * sin_y + sin_one * cos_y).astype(BF16)
    total = dot(field_ref[0], phase_ref[0]) + dot(field_ref[1], phase_ref[1])
    chosen = position == place[2]
    for field in range(fields):
        rows_z = total[field * length : (field + 1) * length]
        picked = jnp.sum(jnp.where(chosen, rows_z, 0.0), axis=0, keepdims=True)
        for unit in range(group):
            out_ref[unit, field : field + 1, :] = picked[:, unit * TB : (unit + 1) * TB]


def sample(ids, packed, field, spectral_shape, units, rows, cols):
    _, comps, vecs, rows_x, rows_y, length = spectral_shape
    group = min(4, units)
    beads = group * TB
    depth = rows_x * rows_y
    count = comps * vecs
    slabs = (length // rows, length // cols)
    return pl.pallas_call(
        functools.partial(sample_kernel, cols, slabs, (rows_x, rows_y)),
        grid=(units // group,),
        out_shape=jax.ShapeDtypeStruct((units, count, TB), F32),
        in_specs=[
            pl.BlockSpec(memory_space=pltpu.SMEM),
            pl.BlockSpec(packed.shape, lambda i: (0, 0, 0)),
            pl.BlockSpec(field.shape, lambda i: (0, 0, 0)),
            pl.BlockSpec((2, length, length), lambda i: (0, 0, 0)),
        ],
        out_specs=pl.BlockSpec((group, count, TB), lambda i: (i, 0, 0)),
        scratch_shapes=[
            pltpu.VMEM((units, 8, TB), F32),
            pltpu.VMEM((2, depth, beads), BF16),
        ],
        compiler_params=pltpu.CompilerParams(vmem_limit_bytes=VMEM_BYTES),
        cost_estimate=pl.CostEstimate(
            flops=2 * 2 * depth * count * length * units * TB,
            bytes_accessed=field.size * 2,
            transcendentals=0,
        ),
        name="sample_far",
    )(ids, packed, field, jnp.asarray(wave_tables(length)))


def near_kernel(units, slots, vecs, ids_ref, packed_ref, kernel_ref, energy_ref, out_ref):
    lanes = vecs * units
    wide = -(-lanes // 128) * 128
    fields = 3 * vecs
    copies = fields + vecs
    group = min(units, 16)
    site = lax.broadcasted_iota(jnp.int32, (SITES, TB), 0)

    lattice = None
    for first in range(0, units, group):
        held, spread = [], []
        for unit in range(first, first + group):
            code = packed_ref[unit, CODE : CODE + 1, :].astype(jnp.int32)
            held.append(jnp.where(site == code, 1.0, 0.0).astype(BF16))
            noise = packed_ref[unit, 0:fields, :]
            high, low = split(noise)
            ones = jnp.ones((vecs, TB), F32)
            pieces = jnp.concatenate(
                [high.astype(F32), ones, low.astype(F32), jnp.zeros((vecs, TB), F32)], axis=0
            )
            mine = lax.broadcasted_iota(jnp.int32, (2 * copies, units, TB), 1) == unit
            block = jnp.where(mine, pieces[:, None, :], 0.0)
            spread.append(block.reshape(2 * copies * units, TB).astype(BF16))
        part = dot_nt(jnp.concatenate(held, axis=1), jnp.concatenate(spread, axis=1))
        lattice = part if lattice is None else lattice + part
    lattice = lattice[:, : copies * units] + lattice[:, copies * units :]
    start = [lanes_from(lattice, lanes * comp, lanes) for comp in range(3)]
    count = lanes_from(lattice, lanes * 3, lanes)

    lane = lax.broadcasted_iota(jnp.int32, (units, wide), 1)
    mix = jnp.zeros((wide, wide), F32)
    row_tiles = packed_ref[:, ROW_TILE, :].astype(jnp.int32)
    col_tiles = packed_ref[:, COL_TILE, :].astype(jnp.int32)
    for slot in range(slots):
        row_unit = row_tiles[:, slot : slot + 1]
        col_unit = col_tiles[:, slot : slot + 1]
        for vec in range(vecs):
            active = row_unit >= 0
            to_row = jnp.where(active & (lane == row_unit + vec * units), 1.0, 0.0).astype(BF16)
            from_col = jnp.where(active & (lane == col_unit + vec * units), 1.0, 0.0).astype(BF16)
            mix = mix + dot_tn(from_col, to_row)
    mix = mix.astype(BF16)

    exact = count.astype(BF16)
    energy = dot(energy_ref[...], jnp.concatenate([exact, exact], axis=0))
    high, low = split(energy)
    energy = dot(high, mix) + dot(low, mix)
    valid = lax.broadcasted_iota(jnp.int32, (SITES, wide), 1) < lanes
    occupied = valid & (count > 0.5)
    largest = jnp.zeros((1, 1), F32)
    for comp in range(3):
        rows = energy[comp * SITES : (comp + 1) * SITES]
        largest = jnp.maximum(largest, jnp.max(jnp.where(occupied, rows, 0.0), keepdims=True))
    scaling = lax.rsqrt(largest + 1e-06)

    def product(vector):
        mixed = [dot(part.astype(BF16), mix).astype(BF16) for part in vector]
        whole = dot(kernel_ref[...], jnp.concatenate(mixed, axis=0))
        return [whole[comp * SITES : (comp + 1) * SITES] for comp in range(3)]

    weights = (
        cheb_coef[1] - cheb_coef[3],
        2.0 * (cheb_coef[2] - cheb_coef[4]),
        2.0 * cheb_coef[3],
        2.0 * cheb_coef[4],
    )
    previous, current = None, start
    total = None
    weight = count * scaling
    for degree in range(4):
        result = product(current)
        scaled = [weights[degree] * part for part in result]
        total = scaled if total is None else [t + s for t, s in zip(total, scaled)]
        if degree < 3:
            if previous is None:
                following = [weight * part for part in result]
            else:
                following = [2.0 * weight * r - p for r, p in zip(result, previous)]
            previous, current = current, following

    me = ids_ref[2]
    code = packed_ref[me, CODE : CODE + 1, :].astype(jnp.int32)
    held = jnp.where(site == code, 1.0, 0.0).astype(BF16)
    noise = packed_ref[me, 0:fields, :]
    row = lax.broadcasted_iota(jnp.int32, (wide, TB), 0)
    rows = []
    for comp in range(3):
        high, low = split(total[comp])
        gathered = dot_tn(high, held) + dot_tn(low, held)
        for vec in range(vecs):
            picked = jnp.where(row == vec * units + me, gathered, 0.0)
            rows.append(jnp.sum(picked, axis=0, keepdims=True))
    near = jnp.concatenate(rows, axis=0) * scaling
    out_ref[...] = (cheb_coef[0] - cheb_coef[2] + cheb_coef[4]) * noise + near


def near(ids, packed, units, slots, vecs):
    kernel_table, energy_table = kernel_tables()
    vmem = pl.BlockSpec(memory_space=pltpu.VMEM)
    return pl.pallas_call(
        functools.partial(near_kernel, units, slots, vecs),
        out_shape=jax.ShapeDtypeStruct((3 * vecs, TB), F32),
        in_specs=[pl.BlockSpec(memory_space=pltpu.SMEM), vmem, vmem, vmem],
        out_specs=vmem,
        compiler_params=pltpu.CompilerParams(vmem_limit_bytes=VMEM_BYTES),
        cost_estimate=pl.CostEstimate(
            flops=4 * 2 * 9 * SITES * SITES * 256, bytes_accessed=8 * 10**6, transcendentals=0
        ),
        name="near_field",
    )(ids, packed, jnp.asarray(kernel_table), jnp.asarray(energy_table))


def per_device(noise_field, offsets, tile_list, send_cells, bead_slot, spectral):
    rows, cols = lax.axis_size("row"), lax.axis_size("col")
    units = rows * cols
    comps, vecs, _ = noise_field.shape
    row_idx, col_idx = lax.axis_index("row"), lax.axis_index("col")
    ids = jnp.stack([row_idx, col_idx, row_idx * cols + col_idx]).astype(jnp.int32)

    def exchange(blocks):
        return lax.all_to_all(blocks, UNIT_AXES, split_axis=0, concat_axis=0, tiled=True)

    packed = exchange(
        pack(ids, noise_field, offsets, tile_list, send_cells, bead_slot, units, cols)
    )
    field = spectrum(ids, spectral)
    partial = exchange(sample(ids, packed, field, spectral.shape, units, rows, cols))
    near_field = near(ids, packed, units, tile_list.shape[3], vecs)
    velocity = near_field + jnp.sum(partial, axis=0)
    return velocity.reshape(comps, vecs, TB)


def solution(mesh):
    return jax.shard_map(
        per_device,
        mesh=mesh,
        in_specs=(
            P(None, None, ("groups", "row", "col")),
            P(None, ("groups", "row", "col")),
            P(("groups", "row"), "col", None, None),
            P(("groups", "row"), "col", None, None),
            P(("groups", "row", "col")),
            P(None, None, None, ("groups", "row"), "col", None),
        ),
        out_specs=P(None, None, ("groups", "row", "col")),
        check_vma=False,
    )
```

```python
import functools
import math

import jax
import jax.numpy as jnp
import ml_dtypes
import numpy as np
from jax import lax
from jax.experimental import pallas as pl
from jax.experimental.pallas import tpu as pltpu
from jax.sharding import PartitionSpec as P

TB = 128
PERIOD = 8
SITES = PERIOD**3
OFFSETS, SLOT, ROW_TILE, COL_TILE, CELLS = 6, 9, 10, 11, 12
UNIT_AXES = ("row", "col")
VMEM_BYTES = 56 * 1024 * 1024

cheb_coef = (1.0, 0.45, -0.2, 0.12, -0.08)
kernel_range = 1.5

F32 = jnp.float32
BF16 = jnp.bfloat16


def kernel_tables():
    ids = np.arange(SITES)
    coords = np.stack([ids // PERIOD**2, ids // PERIOD % PERIOD, ids % PERIOD])
    half = PERIOD // 2
    displace = (coords[:, :, None] - coords[:, None, :] + half) % PERIOD - half
    displace = displace.astype(np.float32)
    squares = (displace * displace).sum(0)
    scale_sq = np.float32(kernel_range * kernel_range)
    envelope = np.exp(squares * np.float32(-0.5 / scale_sq)) / scale_sq
    same, other = [], []
    for left in range(3):
        right = (left + 1) % 3
        same.append(envelope * (displace[left] * displace[left] - squares / np.float32(3.0)))
        other.append(envelope * (displace[left] * displace[right]))
    same = np.stack(same).astype(ml_dtypes.bfloat16)
    other = np.stack(other).astype(ml_dtypes.bfloat16)
    squared = [np.square(t.astype(np.float32)) for t in (same, other)]
    energy = squared[0] + squared[1] + np.roll(squared[1], 1, axis=0)
    high = energy.astype(ml_dtypes.bfloat16)
    low = (energy - high.astype(np.float32)).astype(ml_dtypes.bfloat16)
    return same, other, np.concatenate([high, low], axis=2)


def wave_tables(length):
    ids = np.arange(length)
    angles = (ids[:, None] * ids[None, :] % length) * (2.0 * math.pi / length)
    return np.stack([np.cos(angles), np.sin(angles)]).astype(np.float32)


def last_transform(length):
    cos, sin = wave_tables(length)
    whole = np.concatenate(
        [np.concatenate([cos, -sin], axis=1), np.concatenate([-sin, -cos], axis=1)], axis=0
    )
    return whole.astype(ml_dtypes.bfloat16)


def split(value):
    high = value.astype(BF16)
    return high, (value - high.astype(F32)).astype(BF16)


def quotient(value, by):
    if by & (by - 1) == 0:
        return lax.shift_right_logical(value, int(math.log2(by)))
    return value // by


def remainder(value, by):
    if by & (by - 1) == 0:
        return value & (by - 1)
    return value % by


def dot_nt(left, right):
    return lax.dot_general(left, right, (((1,), (1,)), ((), ())), preferred_element_type=F32)


def dot_tn(left, right):
    return lax.dot_general(left, right, (((0,), (0,)), ((), ())), preferred_element_type=F32)


def dot(left, right):
    return jnp.dot(left, right, preferred_element_type=F32)


def pack_kernel(cols, ids_ref, tiles_ref, noise_ref, offsets_ref, cells_ref, slot_ref, out_ref):
    units = out_ref.shape[0]
    slots = tiles_ref.shape[3]
    lane = lax.broadcasted_iota(jnp.int32, (1, TB), 1)
    row_tile = jnp.full((1, TB), -1, jnp.int32)
    col_tile = jnp.full((1, TB), -1, jnp.int32)
    for slot in range(slots):
        tile_row = tiles_ref[0, 0, 0, slot]
        tile_col = tiles_ref[0, 0, 1, slot]
        active = tile_row >= 0
        row_unit = jnp.where(active, ids_ref[0] * cols + tile_row, -1)
        col_unit = jnp.where(active, tile_col * cols + ids_ref[1], -1)
        row_tile = jnp.where(lane == slot, row_unit, row_tile)
        col_tile = jnp.where(lane == slot, col_unit, col_tile)
    cells = cells_ref[0, 0].astype(F32)
    caps, peers = cells.shape
    if peers < TB:
        cells = jnp.concatenate([cells, jnp.zeros((caps, TB - peers), F32)], axis=1)
        cells = pltpu.roll(cells, 0, 1, stride=peers, stride_axis=0)
        per_row = TB // peers
        cells = jnp.concatenate(
            [
                jnp.sum(cells[at : at + per_row], axis=0, keepdims=True)
                for at in range(0, caps, per_row)
            ],
            axis=0,
        )
    head = [offsets_ref[...], slot_ref[...], row_tile, col_tile]
    block = jnp.concatenate(
        [noise_ref[0], noise_ref[1], noise_ref[2]] + [part.astype(F32) for part in head] + [cells],
        axis=0,
    )
    spare = out_ref.shape[1] - block.shape[0]
    if spare:
        block = jnp.concatenate([block, jnp.zeros((spare, TB), F32)], axis=0)
    for unit in range(units):
        out_ref[unit] = block


def cell_rows(caps, peers):
    per_row = max(1, TB // peers)
    return per_row, -(-caps // per_row)


def pack(ids, noise_field, offsets, tile_list, send_cells, bead_slot, units, cols):
    _, lists = cell_rows(*send_cells.shape[2:])
    rows = -(-(CELLS + lists) // 8) * 8
    vmem = pl.BlockSpec(memory_space=pltpu.VMEM)
    smem = pl.BlockSpec(memory_space=pltpu.SMEM)
    return pl.pallas_call(
        functools.partial(pack_kernel, cols),
        out_shape=jax.ShapeDtypeStruct((units, rows, TB), F32),
        in_specs=[smem, smem, vmem, vmem, vmem, vmem],
        out_specs=vmem,
        name="pack_inputs",
    )(ids, tile_list, noise_field, offsets, send_cells, bead_slot.reshape(1, TB))


def signed(ids, length):
    return jnp.where(ids < length // 2, ids, ids - length).astype(F32)


def spectrum_kernel(rows_x, ids_ref, spec_ref, turn_ref, out_ref):
    _, comps, vecs, part_x, rows_y, length = spec_ref.shape
    shape = (part_x, rows_y, length)
    first_x = ids_ref[0] * rows_x + pl.program_id(0) * part_x
    first_y = ids_ref[1] * rows_y
    wave = (
        signed(first_x + lax.broadcasted_iota(jnp.int32, shape, 0), length),
        signed(first_y + lax.broadcasted_iota(jnp.int32, shape, 1), length),
        signed(lax.broadcasted_iota(jnp.int32, shape, 2), length),
    )
    wave_sq = wave[0] * wave[0] + wave[1] * wave[1] + wave[2] * wave[2]
    width_sq = (length / 8.0) ** 2
    amplitude = jnp.where(
        wave_sq > 0,
        math.sqrt(1.5) / (2.0 * math.pi * width_sq) ** 0.75 * jnp.exp(wave_sq * (-0.25 / width_sq)),
        0.0,
    )
    damped = amplitude / jnp.maximum(wave_sq, 1.0)
    for vec in range(vecs):
        hat = []
        for part in range(2):
            source = [spec_ref[part, comp, vec] for comp in range(comps)]
            along = wave[0] * source[0] + wave[1] * source[1] + wave[2] * source[2]
            factor = along * damped
            hat.append(
                [
                    (amplitude * source[comp] - wave[comp] * factor)
                    .astype(BF16)
                    .reshape(part_x * rows_y, length)
                    for comp in range(comps)
                ]
            )
        for comp in range(comps):
            both = jnp.concatenate([hat[0][comp], hat[1][comp]], axis=1)
            turned = dot_nt(turn_ref[...], both).astype(BF16)
            at = (comp * vecs + vec) * length
            out_ref[0, at : at + length, :] = turned[:length]
            out_ref[1, at : at + length, :] = turned[length:]


def spectrum(ids, spectral):
    _, comps, vecs, rows_x, rows_y, length = spectral.shape
    part_x = max(1, min(rows_x, 256 // rows_y))
    while rows_x % part_x:
        part_x -= 1
    steps = rows_x // part_x
    fields = comps * vecs * length
    return pl.pallas_call(
        functools.partial(spectrum_kernel, rows_x),
        grid=(steps,),
        out_shape=jax.ShapeDtypeStruct((2, fields, rows_x * rows_y), BF16),
        in_specs=[
            pl.BlockSpec(memory_space=pltpu.SMEM),
            pl.BlockSpec((2, comps, vecs, part_x, rows_y, length), lambda i: (0, 0, 0, i, 0, 0)),
            pl.BlockSpec((2 * length, 2 * length), lambda i: (0, 0)),
        ],
        out_specs=pl.BlockSpec((2, fields, part_x * rows_y), lambda i: (0, 0, i)),
        compiler_params=pltpu.CompilerParams(vmem_limit_bytes=VMEM_BYTES),
        cost_estimate=pl.CostEstimate(
            flops=2 * 2 * fields * rows_x * rows_y * 2 * length,
            bytes_accessed=spectral.size * 4 + 4 * fields * rows_x * rows_y,
            transcendentals=rows_x * rows_y * length,
        ),
        name="spectrum",
    )(ids, spectral, jnp.asarray(last_transform(length)))


def find_cells(cols, slabs, per_row, lists, packed_ref, first, group):
    units = packed_ref.shape[0]
    entries = units * lists
    cells = packed_ref[:, CELLS : CELLS + lists, :].reshape(entries, TB).astype(jnp.int32)
    entry = lax.broadcasted_iota(jnp.int32, cells.shape, 0)
    holder = quotient(entry, lists)
    holder_row = quotient(holder, cols)
    holder_col = holder - holder_row * cols
    rest = quotient(cells, slabs[1])
    digits = [
        quotient(rest, slabs[0]),
        holder_row * slabs[0] + remainder(rest, slabs[0]),
        holder_col * slabs[1] + remainder(cells, slabs[1]),
    ]
    digits = jnp.concatenate([d.astype(F32).astype(BF16) for d in digits], axis=1)
    beads = group * TB
    slot = jnp.concatenate(
        [packed_ref[first + unit, SLOT : SLOT + 1, :] for unit in range(group)], axis=1
    ).astype(jnp.int32)
    owner = first + quotient(lax.broadcasted_iota(jnp.int32, (1, beads), 1), TB)
    order = quotient(slot, units)
    index = remainder(slot, units) * lists + quotient(order, per_row)
    lane = remainder(order, per_row) * units + owner
    chosen = lax.broadcasted_iota(jnp.int32, (entries, beads), 0) == index
    found = dot_tn(digits, jnp.where(chosen, 1.0, 0.0).astype(BF16))
    mine = lax.broadcasted_iota(jnp.int32, (TB, beads), 0) == lane
    return [
        jnp.sum(
            jnp.where(mine, found[digit * TB : (digit + 1) * TB], 0.0), axis=0, keepdims=True
        ).astype(jnp.int32)
        for digit in range(3)
    ]


def sample_kernel(
    cols, slabs, rows, lists, group, ids_ref, packed_ref, field_ref, wave_ref, out_ref, phase_ref
):
    length = wave_ref.shape[1]
    comps, vecs = out_ref.shape[1:3]
    beads = group * TB
    position = lax.broadcasted_iota(jnp.int32, (length, beads), 0)
    tables = []
    for axis in range(2):
        first = pl.multiple_of(ids_ref[axis] * rows[axis], rows[axis])
        parts = [split(wave_ref[part, pl.ds(first, rows[axis]), :]) for part in range(2)]
        tables.append(jnp.concatenate([part for pair in parts for part in pair], axis=0))
    rows_y = rows[1]

    def phases(axis, place):
        count = rows[axis]
        chosen = jnp.where(position == place, 1.0, 0.0).astype(BF16)
        found = dot(tables[axis], chosen)
        return [found[2 * p * count : (2 * p + 1) * count] + found[(2 * p + 1) * count : (2 * p + 2) * count] for p in range(2)]

    for part in range(out_ref.shape[0] // group):
        first = pl.program_id(0) * out_ref.shape[0] + part * group
        place = find_cells(cols, slabs, lists[0], lists[1], packed_ref, first, group)
        cos_x, sin_x = phases(0, place[0])
        cos_y, sin_y = [v.astype(BF16) for v in phases(1, place[1])]
        for x in range(rows[0]):
            cos_one = jnp.broadcast_to(cos_x[x : x + 1], (rows_y, beads)).astype(BF16)
            sin_one = jnp.broadcast_to(sin_x[x : x + 1], (rows_y, beads)).astype(BF16)
            at = slice(x * rows_y, (x + 1) * rows_y)
            phase_ref[part % 2, 0, at, :] = cos_one * cos_y - sin_one * sin_y
            phase_ref[part % 2, 1, at, :] = cos_one * sin_y + sin_one * cos_y
        total = dot(field_ref[0], phase_ref[part % 2, 0]) + dot(field_ref[1], phase_ref[part % 2, 1])
        chosen = position == place[2]
        for comp in range(comps):
            for vec in range(vecs):
                at = (comp * vecs + vec) * length
                picked = jnp.where(chosen, total[at : at + length], 0.0)
                picked = jnp.sum(picked, axis=0, keepdims=True)
                for unit in range(group):
                    out_ref[part * group + unit, comp, vec : vec + 1, :] = picked[
                        :, unit * TB : (unit + 1) * TB
                    ]


def sample(ids, packed, field, spectral_shape, cells_shape, rows, cols):
    _, comps, vecs, rows_x, rows_y, length = spectral_shape
    units = rows * cols
    group = 4
    whole = min(16, units)
    depth = rows_x * rows_y
    count = comps * vecs
    slabs = (length // rows, length // cols)
    lists = cell_rows(*cells_shape[2:])
    return pl.pallas_call(
        functools.partial(sample_kernel, cols, slabs, (rows_x, rows_y), lists, group),
        grid=(units // whole,),
        out_shape=jax.ShapeDtypeStruct((units, comps, vecs, TB), F32),
        in_specs=[
            pl.BlockSpec(memory_space=pltpu.SMEM),
            pl.BlockSpec(packed.shape, lambda i: (0, 0, 0)),
            pl.BlockSpec(field.shape, lambda i: (0, 0, 0)),
            pl.BlockSpec((2, length, length), lambda i: (0, 0, 0)),
        ],
        out_specs=pl.BlockSpec((whole, comps, vecs, TB), lambda i: (i, 0, 0, 0)),
        scratch_shapes=[pltpu.VMEM((2, 2, depth, group * TB), BF16)],
        compiler_params=pltpu.CompilerParams(vmem_limit_bytes=VMEM_BYTES),
        cost_estimate=pl.CostEstimate(
            flops=2 * 2 * depth * count * length * units * TB,
            bytes_accessed=field.size * 2,
            transcendentals=0,
        ),
        name="sample_far",
    )(ids, packed, field, jnp.asarray(wave_tables(length)))


def near_kernel(
    units, slots, vecs, ids_ref, packed_ref, same_hbm, other_hbm, energy_hbm, out_ref,
    same_ref, other_ref, energy_ref, rows_ref, sems,
):
    copies = [
        pltpu.make_async_copy(source, target, sems.at[at])
        for at, (source, target) in enumerate(
            [(energy_hbm, energy_ref), (same_hbm, same_ref), (other_hbm, other_ref)]
        )
    ]
    for copy in copies:
        copy.start()

    part = vecs * units
    wide = 4 * part
    fields = 3 * vecs
    group = min(units, 16)
    site = lax.broadcasted_iota(jnp.int32, (SITES, TB), 0)
    block_of = quotient(lax.broadcasted_iota(jnp.int32, (SITES, wide), 1), part)

    def sites_of(unit):
        rows = [packed_ref[unit, OFFSETS + axis : OFFSETS + axis + 1, :] for axis in range(3)]
        code = (rows[0] * PERIOD + rows[1]) * PERIOD + rows[2]
        return jnp.where(site == code.astype(jnp.int32), 1.0, 0.0).astype(BF16)

    lattice = None
    for first in range(0, units, group):
        held, spread = [], []
        for unit in range(first, first + group):
            held.append(sites_of(unit))
            high, low = split(packed_ref[unit, 0:fields, :])
            ones, zeros = jnp.ones((vecs, TB), F32), jnp.zeros((vecs, TB), F32)
            pieces = jnp.concatenate([high.astype(F32), ones, low.astype(F32), zeros], axis=0)
            mine = lax.broadcasted_iota(jnp.int32, (8 * vecs, units, TB), 1) == unit
            block = jnp.where(mine, pieces[:, None, :], 0.0)
            spread.append(block.reshape(2 * wide, TB).astype(BF16))
        term = dot_nt(jnp.concatenate(held, axis=1), jnp.concatenate(spread, axis=1))
        lattice = term if lattice is None else lattice + term
    lattice = lattice[:, :wide] + lattice[:, wide:]
    to_all = lax.broadcasted_iota(jnp.int32, (wide, wide), 0) == 3 * part + remainder(
        lax.broadcasted_iota(jnp.int32, (wide, wide), 1), units
    )
    count = dot(lattice.astype(BF16), jnp.where(to_all, 1.0, 0.0).astype(BF16))

    lane = lax.broadcasted_iota(jnp.int32, (units, wide), 1)
    row_tiles = packed_ref[:, ROW_TILE, :].astype(jnp.int32)
    col_tiles = packed_ref[:, COL_TILE, :].astype(jnp.int32)
    mix = None
    for slot in range(slots):
        row_unit = row_tiles[:, slot : slot + 1]
        col_unit = col_tiles[:, slot : slot + 1]
        active = row_unit >= 0
        from_col, to_row = [], []
        for vec in range(vecs):
            for comp in range(3):

                def hot(unit, at):
                    hit = active & (lane == unit + (at * part + vec * units))
                    return jnp.where(hit, 1.0, 0.0)

                from_col.append(hot(col_unit, comp))
                to_row.append(
                    jnp.concatenate([hot(row_unit, (comp - turn) % 3) for turn in range(3)], axis=1)
                )
        from_col = jnp.concatenate(from_col, axis=0).astype(BF16)
        term = dot_tn(from_col, jnp.concatenate(to_row, axis=0).astype(BF16))
        mix = term if mix is None else mix + term
    mix = mix.astype(BF16)
    mix = jnp.concatenate([mix, mix], axis=0)

    def in_block(block, value):
        return jnp.where(block_of == block, value, 0.0)

    copies[0].wait()
    exact = count.astype(BF16)
    exact = jnp.concatenate([exact, exact], axis=0)
    energy = sum(in_block(comp, dot(energy_ref[comp], exact)) for comp in range(3))
    energy = dot(jnp.concatenate(split(energy), axis=1), mix[:, :wide])
    occupied = (count > 0.5) & (block_of < 3)
    largest = jnp.max(jnp.where(occupied, energy, 0.0), keepdims=True)
    scaling = lax.rsqrt(largest + 1e-06)

    copies[1].wait()
    copies[2].wait()

    def product(vector):
        mixed = dot(jnp.concatenate(split(vector), axis=1), mix).astype(BF16)
        result = None
        for comp in range(3):
            same = dot(same_ref[comp], mixed[:, :wide])
            other = dot(other_ref[comp], mixed[:, wide:])
            term = in_block(comp, same + other[:, :wide]) + in_block(
                (comp + 1) % 3, other[:, wide:]
            )
            result = term if result is None else result + term
        return result

    weights = (
        cheb_coef[1] - cheb_coef[3],
        2.0 * (cheb_coef[2] - cheb_coef[4]),
        2.0 * cheb_coef[3],
        2.0 * cheb_coef[4],
    )
    weight = count * scaling
    previous, current, total = None, lattice, None
    for degree in range(4):
        result = product(current)
        scaled = weights[degree] * result
        total = scaled if total is None else total + scaled
        if degree < 3:
            following = weight * result
            if previous is not None:
                following = 2.0 * following - previous
            previous, current = current, following

    me = ids_ref[2]
    high, low = split(total)
    held = sites_of(me)
    rows_ref[...] = dot_tn(high, held) + dot_tn(low, held)
    first_weight = cheb_coef[0] - cheb_coef[2] + cheb_coef[4]
    for comp in range(3):
        for vec in range(vecs):
            near = rows_ref[pl.ds(comp * part + vec * units + me, 1), :] * scaling
            at = comp * vecs + vec
            noise = packed_ref[me, at : at + 1, :]
            out_ref[comp, vec : vec + 1, :] = first_weight * noise + near


def near(ids, packed, units, slots, vecs):
    tables = [jnp.asarray(table) for table in kernel_tables()]
    vmem = pl.BlockSpec(memory_space=pltpu.VMEM)
    hbm = pl.BlockSpec(memory_space=pl.ANY)
    return pl.pallas_call(
        functools.partial(near_kernel, units, slots, vecs),
        out_shape=jax.ShapeDtypeStruct((3, vecs, TB), F32),
        in_specs=[pl.BlockSpec(memory_space=pltpu.SMEM), vmem, hbm, hbm, hbm],
        out_specs=vmem,
        scratch_shapes=[pltpu.VMEM(table.shape, BF16) for table in tables]
        + [pltpu.VMEM((4 * vecs * units, TB), F32), pltpu.SemaphoreType.DMA((3,))],
        compiler_params=pltpu.CompilerParams(vmem_limit_bytes=VMEM_BYTES),
        cost_estimate=pl.CostEstimate(
            flops=4 * 2 * 9 * SITES * SITES * 256, bytes_accessed=8 * 10**6, transcendentals=0
        ),
        name="near_field",
    )(ids, packed, *tables)


def per_device(noise_field, offsets, tile_list, send_cells, bead_slot, spectral):
    rows, cols = lax.axis_size("row"), lax.axis_size("col")
    units = rows * cols
    vecs = noise_field.shape[1]
    row_idx, col_idx = lax.axis_index("row"), lax.axis_index("col")
    ids = jnp.stack([row_idx, col_idx, row_idx * cols + col_idx]).astype(jnp.int32)

    def exchange(blocks):
        return lax.all_to_all(blocks, UNIT_AXES, split_axis=0, concat_axis=0, tiled=True)

    packed = exchange(
        pack(ids, noise_field, offsets, tile_list, send_cells, bead_slot, units, cols)
    )
    field = spectrum(ids, spectral)
    far = sample(ids, packed, field, spectral.shape, send_cells.shape, rows, cols)
    partial = exchange(far)
    return near(ids, packed, units, tile_list.shape[3], vecs) + jnp.sum(partial, axis=0)


def solution(mesh):
    return jax.shard_map(
        per_device,
        mesh=mesh,
        in_specs=(
            P(None, None, ("groups", "row", "col")),
            P(None, ("groups", "row", "col")),
            P(("groups", "row"), "col", None, None),
            P(("groups", "row"), "col", None, None),
            P(("groups", "row", "col")),
            P(None, None, None, ("groups", "row"), "col", None),
        ),
        out_specs=P(None, None, ("groups", "row", "col")),
        check_vma=False,
    )
```

```python
import functools
import math

import jax
import jax.numpy as jnp
import ml_dtypes
import numpy as np
from jax import lax
from jax.experimental import pallas as pl
from jax.experimental.pallas import tpu as pltpu
from jax.sharding import PartitionSpec as P

TB = 128
PERIOD = 8
SITES = PERIOD**3
PLANE = PERIOD**2
WINDOW = SITES + (PERIOD - 2) * PLANE
OFFSETS, SLOT, ROW_TILE, COL_TILE, CELLS = 6, 9, 10, 11, 12
UNIT_AXES = ("row", "col")
MIB = 1024 * 1024
SPECTRUM_BYTES, SAMPLE_BYTES, NEAR_BYTES = 28 * MIB, 28 * MIB, 28 * MIB

cheb_coef = (1.0, 0.45, -0.2, 0.12, -0.08)
kernel_range = 1.5

F32 = jnp.float32
BF16 = jnp.bfloat16


def kernel_tables():
    ids = np.arange(SITES)
    coords = np.stack([ids // PERIOD**2, ids // PERIOD % PERIOD, ids % PERIOD])
    half = PERIOD // 2
    starts = np.stack([np.arange(WINDOW), np.arange(WINDOW) + PLANE])
    columns = coords[:, starts % SITES]
    displace = (coords[:, None, :PLANE, None] - columns[:, :, None, :] + half) % PERIOD - half
    displace = displace.astype(np.float32)
    squares = (displace * displace).sum(0)
    scale_sq = np.float32(kernel_range * kernel_range)
    envelope = np.exp(squares * np.float32(-0.5 / scale_sq)) / scale_sq
    same, other = [], []
    for left in range(3):
        right = (left + 1) % 3
        same.append(envelope * (displace[left] * displace[left] - squares / np.float32(3.0)))
        other.append(envelope * (displace[left] * displace[right]))
    same = np.stack(same).astype(ml_dtypes.bfloat16)
    other = np.stack(other).astype(ml_dtypes.bfloat16)
    squared = [np.square(t.astype(np.float32)) for t in (same, other)]
    energy = squared[0] + squared[1] + np.roll(squared[1], 1, axis=0)
    high = energy.astype(ml_dtypes.bfloat16)
    low = (energy - high.astype(np.float32)).astype(ml_dtypes.bfloat16)
    return np.stack([same, other]), np.stack([high, low])


def whole_table(ref, kind, comp):
    blocks = []
    for first in range(PERIOD):
        start = -first % PERIOD
        column = (start - start % 2) * PLANE
        blocks.append(ref[kind, comp, start % 2, :, column : column + SITES])
    return jnp.concatenate(blocks, axis=0)


def wave_tables(length):
    ids = np.arange(length)
    angles = (ids[:, None] * ids[None, :] % length) * (2.0 * math.pi / length)
    return np.stack([np.cos(angles), np.sin(angles)]).astype(np.float32)


def last_transform(length):
    cos, sin = wave_tables(length)
    whole = np.concatenate(
        [np.concatenate([cos, -sin], axis=1), np.concatenate([-sin, -cos], axis=1)], axis=0
    )
    return whole.astype(ml_dtypes.bfloat16)


def split(value):
    high = value.astype(BF16)
    return high, (value - high.astype(F32)).astype(BF16)


def quotient(value, by):
    if by & (by - 1) == 0:
        return lax.shift_right_logical(value, int(math.log2(by)))
    return value // by


def remainder(value, by):
    if by & (by - 1) == 0:
        return value & (by - 1)
    return value % by


def dot_nt(left, right):
    return lax.dot_general(left, right, (((1,), (1,)), ((), ())), preferred_element_type=F32)


def dot_tn(left, right):
    return lax.dot_general(left, right, (((0,), (0,)), ((), ())), preferred_element_type=F32)


def dot(left, right):
    return jnp.dot(left, right, preferred_element_type=F32)


def in_hbm(arrays):
    return [pltpu.with_memory_space_constraint(jnp.asarray(a), pltpu.HBM) for a in arrays]


def pack_kernel(cols, tiles_ref, noise_ref, offsets_ref, cells_ref, slot_ref, out_ref):
    units = out_ref.shape[0]
    slots = tiles_ref.shape[3]
    my_row, my_col = lax.axis_index("row"), lax.axis_index("col")
    lane = lax.broadcasted_iota(jnp.int32, (1, TB), 1)
    row_tile = jnp.full((1, TB), -1, jnp.int32)
    col_tile = jnp.full((1, TB), -1, jnp.int32)
    for slot in range(slots):
        tile_row = tiles_ref[0, 0, 0, slot]
        tile_col = tiles_ref[0, 0, 1, slot]
        active = tile_row >= 0
        row_unit = jnp.where(active, my_row * cols + tile_row, -1)
        col_unit = jnp.where(active, tile_col * cols + my_col, -1)
        row_tile = jnp.where(lane == slot, row_unit, row_tile)
        col_tile = jnp.where(lane == slot, col_unit, col_tile)
    cells = cells_ref[0, 0].astype(F32)
    caps, peers = cells.shape
    if peers < TB:
        cells = jnp.concatenate([cells, jnp.zeros((caps, TB - peers), F32)], axis=1)
        cells = pltpu.roll(cells, 0, 1, stride=peers, stride_axis=0)
        per_row = TB // peers
        cells = jnp.concatenate(
            [
                jnp.sum(cells[at : at + per_row], axis=0, keepdims=True)
                for at in range(0, caps, per_row)
            ],
            axis=0,
        )
    head = [offsets_ref[...], slot_ref[...], row_tile, col_tile]
    block = jnp.concatenate(
        [noise_ref[0], noise_ref[1], noise_ref[2]] + [part.astype(F32) for part in head] + [cells],
        axis=0,
    )
    spare = out_ref.shape[1] - block.shape[0]
    if spare:
        block = jnp.concatenate([block, jnp.zeros((spare, TB), F32)], axis=0)
    for unit in range(units):
        out_ref[unit] = block


def cell_rows(caps, peers):
    per_row = max(1, TB // peers)
    return per_row, -(-caps // per_row)


def pack(noise_field, offsets, tile_list, send_cells, bead_slot, units, cols):
    _, lists = cell_rows(*send_cells.shape[2:])
    rows = -(-(CELLS + lists) // 8) * 8
    vmem = pl.BlockSpec(memory_space=pltpu.VMEM)
    smem = pl.BlockSpec(memory_space=pltpu.SMEM)
    return pl.pallas_call(
        functools.partial(pack_kernel, cols),
        out_shape=jax.ShapeDtypeStruct((units, rows, TB), F32),
        in_specs=[smem, vmem, vmem, vmem, vmem],
        out_specs=vmem,
        name="pack_inputs",
    )(tile_list, noise_field, offsets, send_cells, bead_slot.reshape(1, TB))


def signed(ids, length):
    return jnp.where(ids < length // 2, ids, ids - length).astype(F32)


def spectrum_kernel(
    rows_x, spec_hbm, turn_hbm, wave_hbm, out_ref, phase_ref, spec_ref, turn_ref, wave_ref, sems
):
    steps, _, comps, vecs, part_x, rows_y, length = spec_ref.shape
    depth = part_x * rows_y
    shape = (part_x, rows_y, length)
    copies = [
        pltpu.make_async_copy(
            spec_hbm.at[:, :, :, pl.ds(step * part_x, part_x)], spec_ref.at[step], sems.at[step]
        )
        for step in range(steps)
    ]
    tables = [
        pltpu.make_async_copy(source, target, sems.at[steps + at])
        for at, (source, target) in enumerate(
            [(turn_hbm, turn_ref), (wave_hbm, wave_ref)]
        )
    ]
    copies[0].start()
    tables[0].start()
    for copy in copies[1:] + tables[1:]:
        copy.start()
    wave_y = signed(lax.axis_index("col") * rows_y + lax.broadcasted_iota(jnp.int32, shape, 1), length)
    wave_z = signed(lax.broadcasted_iota(jnp.int32, shape, 2), length)
    width_sq = (length / 8.0) ** 2
    height = math.sqrt(1.5) / (2.0 * math.pi * width_sq) ** 0.75
    for step in range(steps):
        first_x = lax.axis_index("row") * rows_x + step * part_x
        wave_x = signed(first_x + lax.broadcasted_iota(jnp.int32, shape, 0), length)
        wave = (wave_x, wave_y, wave_z)
        wave_sq = wave_x * wave_x + wave_y * wave_y + wave_z * wave_z
        amplitude = height * jnp.exp(wave_sq * (-0.25 / width_sq))
        amplitude = jnp.where(wave_sq > 0, amplitude, 0.0)
        damped = amplitude / jnp.maximum(wave_sq, 1.0)
        copies[step].wait()
        if step == 0:
            tables[0].wait()
        for vec in range(vecs):
            hat = []
            for part in range(2):
                source = [spec_ref[step, part, comp, vec] for comp in range(comps)]
                along = wave_x * source[0] + wave_y * source[1] + wave_z * source[2]
                factor = along * damped
                hat.append(
                    [
                        (amplitude * source[comp] - wave[comp] * factor)
                        .astype(BF16)
                        .reshape(depth, length)
                        for comp in range(comps)
                    ]
                )
            for comp in range(comps):
                both = jnp.concatenate([hat[0][comp], hat[1][comp]], axis=1)
                turned = dot_nt(turn_ref[...], both).astype(BF16)
                at = (comp * vecs + vec) * length
                column = 2 * step * depth
                out_ref[at : at + length, column : column + depth] = turned[:length]
                column += depth
                out_ref[at : at + length, column : column + depth] = turned[length:]
    for table in tables[1:]:
        table.wait()
    for axis, count in enumerate((rows_x, rows_y)):
        first = pl.multiple_of(lax.axis_index(UNIT_AXES[axis]) * count, count)
        parts = [split(wave_ref[part, pl.ds(first, count), :]) for part in range(2)]
        parts = [piece for pair in parts for piece in pair]
        phase_ref[axis, 0 : 4 * count, :] = jnp.concatenate(parts, axis=0)


def chunk_of(rows_x, rows_y):
    part_x = max(1, min(rows_x, 256 // rows_y))
    while rows_x % part_x:
        part_x -= 1
    return part_x


def spectrum(spectral):
    _, comps, vecs, rows_x, rows_y, length = spectral.shape
    part_x = chunk_of(rows_x, rows_y)
    steps = rows_x // part_x
    fields = comps * vecs * length
    sources = [spectral, last_transform(length), wave_tables(length)]
    hbm = pl.BlockSpec(memory_space=pltpu.HBM)
    vmem = pl.BlockSpec(memory_space=pltpu.VMEM)
    return pl.pallas_call(
        functools.partial(spectrum_kernel, rows_x),
        out_shape=[
            pltpu.VMEM((fields, 2 * rows_x * rows_y), BF16),
            pltpu.VMEM((2, 4 * max(rows_x, rows_y), length), BF16),
        ],
        in_specs=[hbm] * 3,
        out_specs=[vmem] * 2,
        scratch_shapes=[
            pltpu.VMEM((steps, 2, comps, vecs, part_x, rows_y, length), F32),
            pltpu.VMEM((2 * length, 2 * length), BF16),
            pltpu.VMEM((2, length, length), F32),
            pltpu.SemaphoreType.DMA((steps + 2,)),
        ],
        compiler_params=pltpu.CompilerParams(vmem_limit_bytes=SPECTRUM_BYTES),
        cost_estimate=pl.CostEstimate(
            flops=2 * 2 * fields * rows_x * rows_y * 2 * length,
            bytes_accessed=spectral.size * 4 + 4 * fields * rows_x * rows_y,
            transcendentals=rows_x * rows_y * length,
        ),
        name="spectrum",
    )(*in_hbm(sources))


def find_cells(cols, slabs, per_row, lists, packed_ref, first, group):
    units = packed_ref.shape[0]
    entries = units * lists
    cells = packed_ref[:, CELLS : CELLS + lists, :].reshape(entries, TB).astype(jnp.int32)
    entry = lax.broadcasted_iota(jnp.int32, cells.shape, 0)
    holder = quotient(entry, lists)
    holder_row = quotient(holder, cols)
    holder_col = holder - holder_row * cols
    rest = quotient(cells, slabs[1])
    digits = [
        quotient(rest, slabs[0]),
        holder_row * slabs[0] + remainder(rest, slabs[0]),
        holder_col * slabs[1] + remainder(cells, slabs[1]),
    ]
    digits = jnp.concatenate([d.astype(F32).astype(BF16) for d in digits], axis=1)
    beads = group * TB
    slot = jnp.concatenate(
        [packed_ref[first + unit, SLOT : SLOT + 1, :] for unit in range(group)], axis=1
    ).astype(jnp.int32)
    owner = first + quotient(lax.broadcasted_iota(jnp.int32, (1, beads), 1), TB)
    order = quotient(slot, units)
    index = remainder(slot, units) * lists + quotient(order, per_row)
    lane = remainder(order, per_row) * units + owner
    chosen = lax.broadcasted_iota(jnp.int32, (entries, beads), 0) == index
    found = dot_tn(digits, jnp.where(chosen, 1.0, 0.0).astype(BF16))
    mine = lax.broadcasted_iota(jnp.int32, (TB, beads), 0) == lane
    return [
        jnp.sum(
            jnp.where(mine, found[digit * TB : (digit + 1) * TB], 0.0), axis=0, keepdims=True
        ).astype(jnp.int32)
        for digit in range(3)
    ]


def sample_kernel(
    cols, slabs, rows, lists, groups, packed_ref, field_ref, table_ref, out_ref, *phase_refs
):
    length = table_ref.shape[2]
    comps, vecs = out_ref.shape[1:3]
    rows_y = rows[1]
    part_x = chunk_of(*rows)
    depth = 2 * part_x * rows_y

    def hits(place):
        position = lax.broadcasted_iota(jnp.int32, (length, place.shape[1]), 0)
        return position == place

    def phases(axis, place):
        count = rows[axis]
        found = dot(table_ref[axis, 0 : 4 * count, :], jnp.where(hits(place), 1.0, 0.0).astype(BF16))
        found = [found[at * count : (at + 1) * count] for at in range(4)]
        return found[0] + found[1], found[2] + found[3]

    def fill(first, group, phase_ref):
        first = pl.program_id(0) * out_ref.shape[0] + first
        beads = group * TB
        place = find_cells(cols, slabs, lists[0], lists[1], packed_ref, first, group)
        cos_x, sin_x = phases(0, place[0])
        cos_y, sin_y = [v.astype(BF16) for v in phases(1, place[1])]
        for x in range(rows[0]):
            cos_one = jnp.broadcast_to(cos_x[x : x + 1], (rows_y, beads)).astype(BF16)
            sin_one = jnp.broadcast_to(sin_x[x : x + 1], (rows_y, beads)).astype(BF16)
            at = x // part_x * depth + x % part_x * rows_y
            phase_ref[at : at + rows_y, :] = cos_one * cos_y - sin_one * sin_y
            at += depth // 2
            phase_ref[at : at + rows_y, :] = cos_one * sin_y + sin_one * cos_y
        return place[2]

    def finish(first, group, total, place_z):
        chosen = hits(place_z)
        for comp in range(comps):
            for vec in range(vecs):
                at = (comp * vecs + vec) * length
                picked = jnp.where(chosen, total[at : at + length], 0.0)
                picked = jnp.sum(picked, axis=0, keepdims=True)
                for unit in range(group):
                    out_ref[first + unit, comp, vec : vec + 1, :] = picked[
                        :, unit * TB : (unit + 1) * TB
                    ]

    starts = [sum(groups[:at]) for at in range(len(groups))]
    place_z = fill(0, groups[0], phase_refs[0])
    for at, group in enumerate(groups):
        later = None
        if at + 1 < len(groups):
            later = fill(starts[at + 1], groups[at + 1], phase_refs[at + 1])
        total = dot(field_ref[...], phase_refs[at][...])
        finish(starts[at], group, total, place_z)
        place_z = later


def sample(packed, field, table, spectral_shape, cells_shape, rows, cols):
    _, comps, vecs, rows_x, rows_y, length = spectral_shape
    units = rows * cols
    groups = (2, 6, 8) if units % 16 == 0 else (units,)
    whole = sum(groups)
    depth = rows_x * rows_y
    count = comps * vecs
    slabs = (length // rows, length // cols)
    lists = cell_rows(*cells_shape[2:])
    vmem = pl.BlockSpec(memory_space=pltpu.VMEM)
    return pl.pallas_call(
        functools.partial(sample_kernel, cols, slabs, (rows_x, rows_y), lists, groups),
        grid=(units // whole,),
        out_shape=jax.ShapeDtypeStruct((units, comps, vecs, TB), F32),
        in_specs=[vmem, vmem, vmem],
        out_specs=pl.BlockSpec((whole, comps, vecs, TB), lambda i: (i, 0, 0, 0)),
        scratch_shapes=[pltpu.VMEM((2 * depth, group * TB), BF16) for group in groups],
        compiler_params=pltpu.CompilerParams(vmem_limit_bytes=SAMPLE_BYTES),
        cost_estimate=pl.CostEstimate(
            flops=2 * 2 * depth * count * length * units * TB,
            bytes_accessed=field.size * 2,
            transcendentals=0,
        ),
        name="sample_far",
    )(packed, field, table)


def near_kernel(
    units, cols, slots, vecs, packed_ref, table_hbm, energy_hbm, out_ref,
    table_ref, energy_ref, rows_ref, sems,
):
    copies = [
        pltpu.make_async_copy(table_hbm, table_ref, sems.at[0]),
        pltpu.make_async_copy(energy_hbm, energy_ref, sems.at[1]),
    ]
    for copy in copies:
        copy.start()
    part = vecs * units
    wide = 4 * part
    fields = 3 * vecs
    group = min(units, 16)
    site = lax.broadcasted_iota(jnp.int32, (SITES, TB), 0)
    block_of = quotient(lax.broadcasted_iota(jnp.int32, (SITES, wide), 1), part)

    def sites_of(unit):
        rows = [packed_ref[unit, OFFSETS + axis : OFFSETS + axis + 1, :] for axis in range(3)]
        code = (rows[0] * PERIOD + rows[1]) * PERIOD + rows[2]
        return jnp.where(site == code.astype(jnp.int32), 1.0, 0.0).astype(BF16)

    lattice = None
    for first in range(0, units, group):
        held, spread = [], []
        for unit in range(first, first + group):
            held.append(sites_of(unit))
            high, low = split(packed_ref[unit, 0:fields, :])
            ones, zeros = jnp.ones((vecs, TB), F32), jnp.zeros((vecs, TB), F32)
            pieces = jnp.concatenate([high.astype(F32), ones, low.astype(F32), zeros], axis=0)
            mine = lax.broadcasted_iota(jnp.int32, (8 * vecs, units, TB), 1) == unit
            block = jnp.where(mine, pieces[:, None, :], 0.0)
            spread.append(block.reshape(2 * wide, TB).astype(BF16))
        term = dot_nt(jnp.concatenate(held, axis=1), jnp.concatenate(spread, axis=1))
        lattice = term if lattice is None else lattice + term
    lattice = lattice[:, :wide] + lattice[:, wide:]
    to_all = lax.broadcasted_iota(jnp.int32, (wide, wide), 0) == 3 * part + remainder(
        lax.broadcasted_iota(jnp.int32, (wide, wide), 1), units
    )
    count = dot(lattice.astype(BF16), jnp.where(to_all, 1.0, 0.0).astype(BF16))

    lane = lax.broadcasted_iota(jnp.int32, (units, wide), 1)
    row_tiles = packed_ref[:, ROW_TILE, :].astype(jnp.int32)
    col_tiles = packed_ref[:, COL_TILE, :].astype(jnp.int32)
    mix = None
    for slot in range(slots):
        row_unit = row_tiles[:, slot : slot + 1]
        col_unit = col_tiles[:, slot : slot + 1]
        active = row_unit >= 0
        from_col, to_row = [], []
        for vec in range(vecs):
            for comp in range(3):

                def hot(unit, at):
                    hit = active & (lane == unit + (at * part + vec * units))
                    return jnp.where(hit, 1.0, 0.0)

                from_col.append(hot(col_unit, comp))
                to_row.append(
                    jnp.concatenate([hot(row_unit, (comp - turn) % 3) for turn in range(3)], axis=1)
                )
        from_col = jnp.concatenate(from_col, axis=0).astype(BF16)
        term = dot_tn(from_col, jnp.concatenate(to_row, axis=0).astype(BF16))
        mix = term if mix is None else mix + term
    mix = mix.astype(BF16)
    mix = jnp.concatenate([mix, mix], axis=0)

    def in_block(block, value):
        return jnp.where(block_of == block, value, 0.0)

    for copy in copies:
        copy.wait()

    exact = count.astype(BF16)
    energy = sum(
        in_block(comp, sum(dot(whole_table(energy_ref, kind, comp), exact) for kind in range(2)))
        for comp in range(3)
    )
    energy = dot(jnp.concatenate(split(energy), axis=1), mix[:, :wide])
    occupied = (count > 0.5) & (block_of < 3)
    largest = jnp.max(jnp.where(occupied, energy, 0.0), keepdims=True)
    scaling = lax.rsqrt(largest + 1e-06)

    def product(vector):
        mixed = dot(jnp.concatenate(split(vector), axis=1), mix).astype(BF16)
        result = None
        for comp in range(3):
            same = dot(whole_table(table_ref, 0, comp), mixed[:, :wide])
            other = dot(whole_table(table_ref, 1, comp), mixed[:, wide:])
            term = in_block(comp, same + other[:, :wide]) + in_block(
                (comp + 1) % 3, other[:, wide:]
            )
            result = term if result is None else result + term
        return result

    weights = (
        cheb_coef[1] - cheb_coef[3],
        2.0 * (cheb_coef[2] - cheb_coef[4]),
        2.0 * cheb_coef[3],
        2.0 * cheb_coef[4],
    )
    weight = count * scaling
    previous, current, total = None, lattice, None
    for degree in range(4):
        result = product(current)
        scaled = weights[degree] * result
        total = scaled if total is None else total + scaled
        if degree < 3:
            following = weight * result
            if previous is not None:
                following = 2.0 * following - previous
            previous, current = current, following

    me = lax.axis_index("row") * cols + lax.axis_index("col")
    high, low = split(total)
    held = sites_of(me)
    rows_ref[...] = dot_tn(high, held) + dot_tn(low, held)
    first_weight = cheb_coef[0] - cheb_coef[2] + cheb_coef[4]
    for comp in range(3):
        for vec in range(vecs):
            near = rows_ref[pl.ds(comp * part + vec * units + me, 1), :] * scaling
            at = comp * vecs + vec
            noise = packed_ref[me, at : at + 1, :]
            out_ref[comp, vec : vec + 1, :] = first_weight * noise + near


def near(packed, units, cols, slots, vecs):
    tables = kernel_tables()
    vmem = pl.BlockSpec(memory_space=pltpu.VMEM)
    hbm = pl.BlockSpec(memory_space=pltpu.HBM)
    return pl.pallas_call(
        functools.partial(near_kernel, units, cols, slots, vecs),
        out_shape=pltpu.VMEM((3, vecs, TB), F32),
        in_specs=[vmem] + [hbm] * 2,
        out_specs=vmem,
        scratch_shapes=[pltpu.VMEM(table.shape, BF16) for table in tables]
        + [pltpu.VMEM((4 * vecs * units, TB), F32), pltpu.SemaphoreType.DMA((2,))],
        compiler_params=pltpu.CompilerParams(vmem_limit_bytes=NEAR_BYTES),
        cost_estimate=pl.CostEstimate(
            flops=4 * 2 * 9 * SITES * SITES * 256, bytes_accessed=8 * 10**6, transcendentals=0
        ),
        name="near_field",
    )(packed, *in_hbm(tables))


def per_device(noise_field, offsets, tile_list, send_cells, bead_slot, spectral):
    rows, cols = lax.axis_size("row"), lax.axis_size("col")
    units = rows * cols
    vecs = noise_field.shape[1]

    def exchange(blocks):
        return lax.all_to_all(blocks, UNIT_AXES, split_axis=0, concat_axis=0, tiled=True)

    packed = exchange(
        pack(noise_field, offsets, tile_list, send_cells, bead_slot, units, cols)
    )
    field, waves = spectrum(spectral)
    far = sample(packed, field, waves, spectral.shape, send_cells.shape, rows, cols)
    partial = exchange(far)
    near_field = near(packed, units, cols, tile_list.shape[3], vecs)
    return near_field + jnp.sum(partial, axis=0)


def solution(mesh):
    return jax.shard_map(
        per_device,
        mesh=mesh,
        in_specs=(
            P(None, None, ("groups", "row", "col")),
            P(None, ("groups", "row", "col")),
            P(("groups", "row"), "col", None, None),
            P(("groups", "row"), "col", None, None),
            P(("groups", "row", "col")),
            P(None, None, None, ("groups", "row"), "col", None),
        ),
        out_specs=P(None, None, ("groups", "row", "col")),
        check_vma=False,
    )
```

```python
import functools
import math

import jax
import jax.numpy as jnp
import ml_dtypes
import numpy as np
from jax import lax
from jax.experimental import pallas as pl
from jax.experimental.pallas import tpu as pltpu
from jax.sharding import PartitionSpec as P

TB = 128
PERIOD = 8
SITES = PERIOD**3
PLANE = PERIOD**2
WINDOW = SITES + (PERIOD - 2) * PLANE
HALVED = SITES // 2
OFFSETS, SLOT, TILES, CELLS = 6, 9, 10, 11
HALF = 256
UNIT_AXES = ("row", "col")
MIB = 1024 * 1024
SPECTRUM_BYTES, SAMPLE_BYTES, NEAR_BYTES = 28 * MIB, 28 * MIB, 50 * MIB

cheb_coef = (1.0, 0.45, -0.2, 0.12, -0.08)
kernel_range = 1.5

F32 = jnp.float32
BF16 = jnp.bfloat16


def kernel_tables():
    ids = np.arange(SITES)
    coords = np.stack([ids // PERIOD**2, ids // PERIOD % PERIOD, ids % PERIOD])
    half = PERIOD // 2
    displace = (coords[:, :, None] - coords[:, None, :] + half) % PERIOD - half
    displace = displace.astype(np.float32)
    squares = (displace * displace).sum(0)
    scale_sq = np.float32(kernel_range * kernel_range)
    envelope = np.exp(squares * np.float32(-0.5 / scale_sq)) / scale_sq
    same, other = [], []
    for left in range(3):
        right = (left + 1) % 3
        same.append(envelope * (displace[left] * displace[left] - squares / np.float32(3.0)))
        other.append(envelope * (displace[left] * displace[right]))
    same = np.stack(same).astype(ml_dtypes.bfloat16)
    other = np.stack(other).astype(ml_dtypes.bfloat16)
    squared = [np.square(t.astype(np.float32)) for t in (same, other)]
    energy = squared[0] + squared[1] + np.roll(squared[1], 1, axis=0)
    columns = (np.arange(WINDOW)[None, :] + np.array([[0], [PLANE]])) % SITES
    rows = np.stack([same, other])[:, :, :PLANE]
    windows = np.stack([rows[..., shifted] for shifted in columns], axis=2)
    first, last = energy[:, :HALVED, :HALVED], energy[:, :HALVED, HALVED:]
    halves = 0.5 * np.stack([first + last, first - last], axis=1)
    high = halves.astype(ml_dtypes.bfloat16)
    low = (halves - high.astype(np.float32)).astype(ml_dtypes.bfloat16)
    return windows, np.concatenate([high, low], axis=3)


def whole_table(ref, kind, comp):
    blocks = []
    for first in range(PERIOD):
        start = -first % PERIOD
        column = (start - start % 2) * PLANE
        blocks.append(ref[kind, comp, start % 2, :, column : column + SITES])
    return jnp.concatenate(blocks, axis=0)


def wave_tables(length):
    ids = np.arange(length)
    angles = (ids[:, None] * ids[None, :] % length) * (2.0 * math.pi / length)
    return np.stack([np.cos(angles), np.sin(angles)]).astype(np.float32)


def last_transform(length):
    cos, sin = wave_tables(length)
    whole = np.concatenate(
        [np.concatenate([cos, -sin], axis=1), np.concatenate([-sin, -cos], axis=1)], axis=0
    )
    return whole.astype(ml_dtypes.bfloat16)


def split(value):
    high = value.astype(BF16)
    return high, (value - high.astype(F32)).astype(BF16)


def quotient(value, by):
    if by & (by - 1) == 0:
        return lax.shift_right_logical(value, int(math.log2(by)))
    return value // by


def remainder(value, by):
    if by & (by - 1) == 0:
        return value & (by - 1)
    return value % by


def dot_nt(left, right):
    return lax.dot_general(left, right, (((1,), (1,)), ((), ())), preferred_element_type=F32)


def dot_tn(left, right):
    return lax.dot_general(left, right, (((0,), (0,)), ((), ())), preferred_element_type=F32)


def dot(left, right):
    return jnp.dot(left, right, preferred_element_type=F32)


def in_hbm(arrays):
    return [pltpu.with_memory_space_constraint(jnp.asarray(a), pltpu.HBM) for a in arrays]


def pack_kernel(cols, tiles_ref, noise_ref, offsets_ref, cells_ref, slot_ref, out_ref):
    units = out_ref.shape[0]
    slots = tiles_ref.shape[3]
    my_row, my_col = lax.axis_index("row"), lax.axis_index("col")
    lane = lax.broadcasted_iota(jnp.int32, (1, TB), 1)
    tiles = jnp.full((1, TB), -1, jnp.int32)
    for slot in range(slots):
        tile_row = tiles_ref[0, 0, 0, slot]
        tile_col = tiles_ref[0, 0, 1, slot]
        active = tile_row >= 0
        row_unit = jnp.where(active, my_row * cols + tile_row, -1)
        col_unit = jnp.where(active, tile_col * cols + my_col, -1)
        tiles = jnp.where(lane == slot, row_unit, tiles)
        tiles = jnp.where(lane == slot + TB // 2, col_unit, tiles)
    cells = cells_ref[0, 0].astype(F32)
    caps, peers = cells.shape
    if peers < TB:
        cells = jnp.concatenate([cells, jnp.zeros((caps, TB - peers), F32)], axis=1)
        cells = pltpu.roll(cells, 0, 1, stride=peers, stride_axis=0)
        per_row = TB // peers
        cells = jnp.concatenate(
            [
                jnp.sum(cells[at : at + per_row], axis=0, keepdims=True)
                for at in range(0, caps, per_row)
            ],
            axis=0,
        )
    cells = cells.astype(jnp.int32)
    head = [offsets_ref[...], slot_ref[...], tiles]
    head += [quotient(cells, 2 * HALF), remainder(cells, 2 * HALF) - HALF]
    block = jnp.concatenate(
        [noise_ref[0], noise_ref[1], noise_ref[2]] + [part.astype(F32) for part in head], axis=0
    )
    spare = out_ref.shape[1] - block.shape[0]
    if spare:
        block = jnp.concatenate([block, jnp.zeros((spare, TB), F32)], axis=0)
    block = block.astype(BF16)
    for unit in range(units):
        out_ref[unit] = block


def cell_rows(caps, peers):
    per_row = max(1, TB // peers)
    return per_row, -(-caps // per_row)


def pack(noise_field, offsets, tile_list, send_cells, bead_slot, units, cols):
    _, lists = cell_rows(*send_cells.shape[2:])
    rows = -(-(CELLS + 2 * lists) // 16) * 16
    vmem = pl.BlockSpec(memory_space=pltpu.VMEM)
    smem = pl.BlockSpec(memory_space=pltpu.SMEM)
    return pl.pallas_call(
        functools.partial(pack_kernel, cols),
        out_shape=jax.ShapeDtypeStruct((units, rows, TB), BF16),
        in_specs=[smem, vmem, vmem, vmem, vmem],
        out_specs=vmem,
        name="pack_inputs",
    )(tile_list, noise_field, offsets, send_cells, bead_slot.reshape(1, TB))


def signed(ids, length):
    return jnp.where(ids < length // 2, ids, ids - length).astype(F32)


def spectrum_kernel(
    rows_x, spec_hbm, turn_hbm, wave_hbm, out_ref, phase_ref, spec_ref, turn_ref, wave_ref, sems
):
    steps, _, comps, vecs, part_x, rows_y, length = spec_ref.shape
    depth = part_x * rows_y
    shape = (part_x, rows_y, length)
    copies = [
        pltpu.make_async_copy(
            spec_hbm.at[:, :, :, pl.ds(step * part_x, part_x)], spec_ref.at[step], sems.at[step]
        )
        for step in range(steps)
    ]
    tables = [
        pltpu.make_async_copy(source, target, sems.at[steps + at])
        for at, (source, target) in enumerate(
            [(turn_hbm, turn_ref), (wave_hbm, wave_ref)]
        )
    ]
    copies[0].start()
    tables[0].start()
    for copy in copies[1:] + tables[1:]:
        copy.start()
    wave_y = signed(lax.axis_index("col") * rows_y + lax.broadcasted_iota(jnp.int32, shape, 1), length)
    wave_z = signed(lax.broadcasted_iota(jnp.int32, shape, 2), length)
    width_sq = (length / 8.0) ** 2
    height = math.sqrt(1.5) / (2.0 * math.pi * width_sq) ** 0.75
    for step in range(steps):
        first_x = lax.axis_index("row") * rows_x + step * part_x
        wave_x = signed(first_x + lax.broadcasted_iota(jnp.int32, shape, 0), length)
        wave = (wave_x, wave_y, wave_z)
        wave_sq = wave_x * wave_x + wave_y * wave_y + wave_z * wave_z
        amplitude = height * jnp.exp(wave_sq * (-0.25 / width_sq))
        amplitude = jnp.where(wave_sq > 0, amplitude, 0.0)
        damped = amplitude / jnp.maximum(wave_sq, 1.0)
        copies[step].wait()
        if step == 0:
            tables[0].wait()
        for vec in range(vecs):
            hat = []
            for part in range(2):
                source = [spec_ref[step, part, comp, vec] for comp in range(comps)]
                along = wave_x * source[0] + wave_y * source[1] + wave_z * source[2]
                factor = along * damped
                hat.append(
                    [
                        (amplitude * source[comp] - wave[comp] * factor)
                        .astype(BF16)
                        .reshape(depth, length)
                        for comp in range(comps)
                    ]
                )
            for comp in range(comps):
                both = jnp.concatenate([hat[0][comp], hat[1][comp]], axis=1)
                turned = dot_nt(turn_ref[...], both).astype(BF16)
                at = (comp * vecs + vec) * length
                column = 2 * step * depth
                out_ref[at : at + length, column : column + depth] = turned[:length]
                column += depth
                out_ref[at : at + length, column : column + depth] = turned[length:]
    for table in tables[1:]:
        table.wait()
    for axis, count in enumerate((rows_x, rows_y)):
        first = pl.multiple_of(lax.axis_index(UNIT_AXES[axis]) * count, count)
        parts = [split(wave_ref[part, pl.ds(first, count), :]) for part in range(2)]
        parts = [piece for pair in parts for piece in pair]
        phase_ref[axis, 0 : 4 * count, :] = jnp.concatenate(parts, axis=0)


def chunk_of(rows_x, rows_y):
    part_x = max(1, min(rows_x, 256 // rows_y))
    while rows_x % part_x:
        part_x -= 1
    return part_x


def spectrum(spectral):
    _, comps, vecs, rows_x, rows_y, length = spectral.shape
    part_x = chunk_of(rows_x, rows_y)
    steps = rows_x // part_x
    fields = comps * vecs * length
    sources = [spectral, last_transform(length), wave_tables(length)]
    hbm = pl.BlockSpec(memory_space=pltpu.HBM)
    vmem = pl.BlockSpec(memory_space=pltpu.VMEM)
    return pl.pallas_call(
        functools.partial(spectrum_kernel, rows_x),
        out_shape=[
            pltpu.VMEM((fields, 2 * rows_x * rows_y), BF16),
            pltpu.VMEM((2, 4 * max(rows_x, rows_y), length), BF16),
        ],
        in_specs=[hbm] * 3,
        out_specs=[vmem] * 2,
        scratch_shapes=[
            pltpu.VMEM((steps, 2, comps, vecs, part_x, rows_y, length), F32),
            pltpu.VMEM((2 * length, 2 * length), BF16),
            pltpu.VMEM((2, length, length), F32),
            pltpu.SemaphoreType.DMA((steps + 2,)),
        ],
        compiler_params=pltpu.CompilerParams(vmem_limit_bytes=SPECTRUM_BYTES),
        cost_estimate=pl.CostEstimate(
            flops=2 * 2 * fields * rows_x * rows_y * 2 * length,
            bytes_accessed=spectral.size * 4 + 4 * fields * rows_x * rows_y,
            transcendentals=rows_x * rows_y * length,
        ),
        name="spectrum",
    )(*in_hbm(sources))


def find_cells(cols, slabs, per_row, lists, packed_ref, first, group):
    units = packed_ref.shape[0]
    entries = units * lists
    packed = packed_ref[...].astype(F32)
    high = packed[:, CELLS : CELLS + lists, :].reshape(entries, TB)
    low = packed[:, CELLS + lists : CELLS + 2 * lists, :].reshape(entries, TB)
    cells = (high * (2 * HALF) + (low + HALF)).astype(jnp.int32)
    entry = lax.broadcasted_iota(jnp.int32, cells.shape, 0)
    holder = quotient(entry, lists)
    holder_row = quotient(holder, cols)
    holder_col = holder - holder_row * cols
    rest = quotient(cells, slabs[1])
    digits = [
        quotient(rest, slabs[0]),
        holder_row * slabs[0] + remainder(rest, slabs[0]),
        holder_col * slabs[1] + remainder(cells, slabs[1]),
    ]
    digits = jnp.concatenate([d.astype(F32).astype(BF16) for d in digits], axis=1)
    beads = group * TB
    slot = jnp.concatenate(
        [packed_ref[first + unit].astype(F32)[SLOT : SLOT + 1] for unit in range(group)], axis=1
    ).astype(jnp.int32)
    owner = first + quotient(lax.broadcasted_iota(jnp.int32, (1, beads), 1), TB)
    order = quotient(slot, units)
    index = remainder(slot, units) * lists + quotient(order, per_row)
    lane = remainder(order, per_row) * units + owner
    chosen = lax.broadcasted_iota(jnp.int32, (entries, beads), 0) == index
    found = dot_tn(digits, jnp.where(chosen, 1.0, 0.0).astype(BF16))
    mine = lax.broadcasted_iota(jnp.int32, (TB, beads), 0) == lane
    return [
        jnp.sum(
            jnp.where(mine, found[digit * TB : (digit + 1) * TB], 0.0), axis=0, keepdims=True
        ).astype(jnp.int32)
        for digit in range(3)
    ]


def sample_kernel(
    cols, slabs, rows, lists, groups, packed_ref, field_ref, table_ref, out_ref, *phase_refs
):
    length = table_ref.shape[2]
    comps, vecs = out_ref.shape[1:3]
    rows_y = rows[1]
    part_x = chunk_of(*rows)
    depth = 2 * part_x * rows_y

    def hits(place):
        position = lax.broadcasted_iota(jnp.int32, (length, place.shape[1]), 0)
        return position == place

    def phases(axis, place):
        count = rows[axis]
        found = dot(table_ref[axis, 0 : 4 * count, :], jnp.where(hits(place), 1.0, 0.0).astype(BF16))
        found = [found[at * count : (at + 1) * count] for at in range(4)]
        return found[0] + found[1], found[2] + found[3]

    def fill(first, group, phase_ref):
        first = pl.program_id(0) * out_ref.shape[0] + first
        beads = group * TB
        place = find_cells(cols, slabs, lists[0], lists[1], packed_ref, first, group)
        cos_x, sin_x = phases(0, place[0])
        cos_y, sin_y = [v.astype(BF16) for v in phases(1, place[1])]
        for x in range(rows[0]):
            cos_one = jnp.broadcast_to(cos_x[x : x + 1], (rows_y, beads)).astype(BF16)
            sin_one = jnp.broadcast_to(sin_x[x : x + 1], (rows_y, beads)).astype(BF16)
            at = x // part_x * depth + x % part_x * rows_y
            phase_ref[at : at + rows_y, :] = cos_one * cos_y - sin_one * sin_y
            at += depth // 2
            phase_ref[at : at + rows_y, :] = cos_one * sin_y + sin_one * cos_y
        return place[2]

    def finish(first, group, total, place_z):
        chosen = hits(place_z)
        for comp in range(comps):
            for vec in range(vecs):
                at = (comp * vecs + vec) * length
                picked = jnp.where(chosen, total[at : at + length], 0.0)
                picked = jnp.sum(picked, axis=0, keepdims=True)
                for unit in range(group):
                    out_ref[first + unit, comp, vec : vec + 1, :] = picked[
                        :, unit * TB : (unit + 1) * TB
                    ]

    starts = [sum(groups[:at]) for at in range(len(groups))]
    place_z = fill(0, groups[0], phase_refs[0])
    for at, group in enumerate(groups):
        later = None
        if at + 1 < len(groups):
            later = fill(starts[at + 1], groups[at + 1], phase_refs[at + 1])
        total = dot(field_ref[...], phase_refs[at][...])
        finish(starts[at], group, total, place_z)
        place_z = later


def sample(packed, field, table, spectral_shape, cells_shape, rows, cols):
    _, comps, vecs, rows_x, rows_y, length = spectral_shape
    units = rows * cols
    groups = (2, 6, 8) if units % 16 == 0 else (units,)
    whole = sum(groups)
    depth = rows_x * rows_y
    count = comps * vecs
    slabs = (length // rows, length // cols)
    lists = cell_rows(*cells_shape[2:])
    vmem = pl.BlockSpec(memory_space=pltpu.VMEM)
    return pl.pallas_call(
        functools.partial(sample_kernel, cols, slabs, (rows_x, rows_y), lists, groups),
        grid=(units // whole,),
        out_shape=jax.ShapeDtypeStruct((units, comps, vecs, TB), F32),
        in_specs=[vmem] * 3,
        out_specs=pl.BlockSpec((whole, comps, vecs, TB), lambda i: (i, 0, 0, 0)),
        scratch_shapes=[pltpu.VMEM((2 * depth, group * TB), BF16) for group in groups],
        compiler_params=pltpu.CompilerParams(vmem_limit_bytes=SAMPLE_BYTES),
        cost_estimate=pl.CostEstimate(
            flops=2 * 2 * depth * count * length * units * TB,
            bytes_accessed=field.size * 2,
            transcendentals=0,
        ),
        name="sample_far",
    )(packed, field, table)


def over(count, term, sum_refs):
    if not sum_refs:
        return functools.reduce(lambda a, b: a + b, [term(at) for at in range(count)])
    sum_ref = sum_refs[0]
    sum_ref[...] = term(0)

    def step(at, carry):
        sum_ref[...] += term(at)
        return carry

    lax.fori_loop(1, count, step, 0)
    return sum_ref[...]


def near_kernel(
    units, cols, slots, vecs, packed_ref, noise_ref, table_hbm, energy_hbm, out_ref,
    table_ref, energy_ref, rows_ref, sems, *sum_refs,
):
    copies = [
        pltpu.make_async_copy(table_hbm, table_ref, sems.at[0]),
        pltpu.make_async_copy(energy_hbm, energy_ref, sems.at[1]),
    ]
    for copy in copies:
        copy.start()

    part = vecs * units
    wide = 4 * part
    fields = 3 * vecs
    group = min(units, 16)
    site = lax.broadcasted_iota(jnp.int32, (SITES, TB), 0)
    block_of = quotient(lax.broadcasted_iota(jnp.int32, (SITES, wide), 1), part)

    def sites_of(unit):
        rows = packed_ref[unit].astype(F32)[OFFSETS : OFFSETS + 3]
        code = (rows[0:1] * PERIOD + rows[1:2]) * PERIOD + rows[2:3]
        return jnp.where(site == code.astype(jnp.int32), 1.0, 0.0).astype(BF16)

    def scatter(first):
        held, spread = [], []
        for at in range(group):
            unit = first + at
            held.append(sites_of(unit))
            noise = packed_ref[unit].astype(F32)[0:fields]
            pieces = jnp.concatenate([noise, jnp.ones((vecs, TB), F32)], axis=0)
            mine = lax.broadcasted_iota(jnp.int32, (4 * vecs, units, TB), 1) == unit
            block = jnp.where(mine, pieces[:, None, :], 0.0)
            spread.append(block.reshape(wide, TB).astype(BF16))
        return dot_nt(jnp.concatenate(held, axis=1), jnp.concatenate(spread, axis=1))

    lattice = over(units // group, lambda at: scatter(at * group), sum_refs[:1])
    to_all = lax.broadcasted_iota(jnp.int32, (wide, wide), 0) == 3 * part + remainder(
        lax.broadcasted_iota(jnp.int32, (wide, wide), 1), units
    )
    count = dot(lattice.astype(BF16), jnp.where(to_all, 1.0, 0.0).astype(BF16))

    lane = lax.broadcasted_iota(jnp.int32, (units, wide), 1)
    tiles = packed_ref[...].astype(F32)[:, TILES, :].astype(jnp.int32)
    tile_lane = lax.broadcasted_iota(jnp.int32, (units, TB), 1)

    def links(slot):
        row_unit, col_unit = [
            jnp.sum(jnp.where(tile_lane == slot + start, tiles, 0), axis=1, keepdims=True)
            for start in (0, TB // 2)
        ]
        active = row_unit >= 0
        from_col, to_row = [], []
        for vec in range(vecs):
            for comp in range(3):

                def hot(unit, at):
                    hit = active & (lane == unit + (at * part + vec * units))
                    return jnp.where(hit, 1.0, 0.0)

                from_col.append(hot(col_unit, comp))
                to_row.append(
                    jnp.concatenate([hot(row_unit, (comp - turn) % 3) for turn in range(3)], axis=1)
                )
        from_col = jnp.concatenate(from_col, axis=0).astype(BF16)
        return dot_tn(from_col, jnp.concatenate(to_row, axis=0).astype(BF16))

    mix = over(slots, links, sum_refs[1:])
    mix = mix.astype(BF16)
    mix = jnp.concatenate([mix, mix], axis=0)

    def in_block(block, value):
        return jnp.where(block_of == block, value, 0.0)

    for copy in copies:
        copy.wait()

    halves = (count[:HALVED] + count[HALVED:], count[:HALVED] - count[HALVED:])
    halves = [jnp.concatenate([half.astype(BF16)] * 2, axis=0) for half in halves]
    energy = None
    for comp in range(3):
        plus, minus = [dot(energy_ref[comp, kind], half) for kind, half in enumerate(halves)]
        term = in_block(comp, jnp.concatenate([plus + minus, plus - minus], axis=0))
        energy = term if energy is None else energy + term
    energy = dot(jnp.concatenate(split(energy), axis=1), mix[:, :wide])
    occupied = (count > 0.5) & (block_of < 3)
    largest = jnp.max(jnp.where(occupied, energy, 0.0), keepdims=True)
    scaling = lax.rsqrt(largest + 1e-06)

    def product(vector):
        mixed = dot(jnp.concatenate(split(vector), axis=1), mix).astype(BF16)
        result = None
        for comp in range(3):
            same = dot(whole_table(table_ref, 0, comp), mixed[:, :wide])
            other = dot(whole_table(table_ref, 1, comp), mixed[:, wide:])
            term = in_block(comp, same + other[:, :wide]) + in_block(
                (comp + 1) % 3, other[:, wide:]
            )
            result = term if result is None else result + term
        return result

    weights = (
        cheb_coef[1] - cheb_coef[3],
        2.0 * (cheb_coef[2] - cheb_coef[4]),
        2.0 * cheb_coef[3],
        2.0 * cheb_coef[4],
    )
    weight = count * scaling
    previous, current, total = None, lattice, None
    for degree in range(4):
        result = product(current)
        scaled = weights[degree] * result
        total = scaled if total is None else total + scaled
        if degree < 3:
            following = weight * result
            if previous is not None:
                following = 2.0 * following - previous
            previous, current = current, following

    me = lax.axis_index("row") * cols + lax.axis_index("col")
    high, low = split(total)
    held = sites_of(me)
    rows_ref[...] = dot_tn(high, held) + dot_tn(low, held)
    first_weight = cheb_coef[0] - cheb_coef[2] + cheb_coef[4]
    for comp in range(3):
        for vec in range(vecs):
            near = rows_ref[pl.ds(comp * part + vec * units + me, 1), :] * scaling
            out_ref[comp, vec : vec + 1, :] = first_weight * noise_ref[comp, vec : vec + 1, :] + near


def near(packed, noise_field, units, cols, slots):
    vecs = noise_field.shape[1]
    wide = 4 * vecs * units
    tables = kernel_tables()
    vmem = pl.BlockSpec(memory_space=pltpu.VMEM)
    hbm = pl.BlockSpec(memory_space=pltpu.HBM)
    sums = [(SITES, wide), (wide, 3 * wide)] if units > 16 else []
    return pl.pallas_call(
        functools.partial(near_kernel, units, cols, slots, vecs),
        out_shape=pltpu.VMEM((3, vecs, TB), F32),
        in_specs=[vmem] * 2 + [hbm] * 2,
        out_specs=vmem,
        scratch_shapes=[pltpu.VMEM(table.shape, BF16) for table in tables]
        + [pltpu.VMEM((wide, TB), F32), pltpu.SemaphoreType.DMA((2,))]
        + [pltpu.VMEM(shape, F32) for shape in sums],
        compiler_params=pltpu.CompilerParams(vmem_limit_bytes=NEAR_BYTES),
        cost_estimate=pl.CostEstimate(
            flops=4 * 2 * 9 * SITES * SITES * 256, bytes_accessed=8 * 10**6, transcendentals=0
        ),
        name="near_field",
    )(packed, noise_field, *in_hbm(tables))


def per_device(noise_field, offsets, tile_list, send_cells, bead_slot, spectral):
    rows, cols = lax.axis_size("row"), lax.axis_size("col")
    units = rows * cols

    def exchange(blocks):
        return lax.all_to_all(blocks, UNIT_AXES, split_axis=0, concat_axis=0, tiled=True)

    packed = exchange(
        pack(noise_field, offsets, tile_list, send_cells, bead_slot, units, cols)
    )
    field, waves = spectrum(spectral)
    far = sample(packed, field, waves, spectral.shape, send_cells.shape, rows, cols)
    partial = exchange(far)
    near_field = near(packed, noise_field, units, cols, tile_list.shape[3])
    return near_field + jnp.sum(partial, axis=0)


def solution(mesh):
    return jax.shard_map(
        per_device,
        mesh=mesh,
        in_specs=(
            P(None, None, ("groups", "row", "col")),
            P(None, ("groups", "row", "col")),
            P(("groups", "row"), "col", None, None),
            P(("groups", "row"), "col", None, None),
            P(("groups", "row", "col")),
            P(None, None, None, ("groups", "row"), "col", None),
        ),
        out_specs=P(None, None, ("groups", "row", "col")),
        check_vma=False,
    )
```

```python
import functools
import math

import jax
import jax.numpy as jnp
import ml_dtypes
import numpy as np
from jax import lax
from jax.experimental import pallas as pl
from jax.experimental.pallas import tpu as pltpu
from jax.sharding import PartitionSpec as P

TB = 128
PERIOD = 8
SITES = PERIOD**3
PLANE = PERIOD**2
WINDOW = SITES + (PERIOD - 2) * PLANE
HALVED = SITES // 2
OFFSETS, SLOT, TILES, CELLS = 6, 9, 10, 11
HALF = 256
UNIT_AXES = ("row", "col")
MIB = 1024 * 1024
SPECTRUM_BYTES, SAMPLE_BYTES, NEAR_BYTES = 28 * MIB, 28 * MIB, 50 * MIB

cheb_coef = (1.0, 0.45, -0.2, 0.12, -0.08)
kernel_range = 1.5

F32 = jnp.float32
BF16 = jnp.bfloat16


def kernel_tables():
    ids = np.arange(SITES)
    coords = np.stack([ids // PERIOD**2, ids // PERIOD % PERIOD, ids % PERIOD])
    half = PERIOD // 2
    displace = (coords[:, :, None] - coords[:, None, :] + half) % PERIOD - half
    displace = displace.astype(np.float32)
    squares = (displace * displace).sum(0)
    scale_sq = np.float32(kernel_range * kernel_range)
    envelope = np.exp(squares * np.float32(-0.5 / scale_sq)) / scale_sq
    same, other = [], []
    for left in range(3):
        right = (left + 1) % 3
        same.append(envelope * (displace[left] * displace[left] - squares / np.float32(3.0)))
        other.append(envelope * (displace[left] * displace[right]))
    same = np.stack(same).astype(ml_dtypes.bfloat16)
    other = np.stack(other).astype(ml_dtypes.bfloat16)
    squared = [np.square(t.astype(np.float32)) for t in (same, other)]
    energy = squared[0] + squared[1] + np.roll(squared[1], 1, axis=0)
    columns = (np.arange(WINDOW)[None, :] + np.array([[0], [PLANE]])) % SITES
    rows = np.stack([same, other])[:, :, :PLANE]
    windows = np.stack([rows[..., shifted] for shifted in columns], axis=2)
    energy_halves = halved_tables(energy)
    pair_halves = halved_tables(np.stack([same, other]).astype(np.float32))[0]
    pair_halves = np.moveaxis(pair_halves, 2, 1).reshape(2, 2, 3 * HALVED, HALVED)
    return windows, np.concatenate(energy_halves, axis=3), pair_halves


def halved_tables(tables):
    first, last = tables[..., :HALVED, :HALVED], tables[..., :HALVED, HALVED:]
    halves = 0.5 * np.stack([first + last, first - last], axis=-3)
    high = halves.astype(ml_dtypes.bfloat16)
    return high, (halves - high.astype(np.float32)).astype(ml_dtypes.bfloat16)


def halve(value):
    return value[:HALVED] + value[HALVED:], value[:HALVED] - value[HALVED:]


def unhalve(plus, minus):
    return jnp.concatenate([plus + minus, plus - minus], axis=0)


def whole_table(ref, kind, comp):
    blocks = []
    for first in range(PERIOD):
        start = -first % PERIOD
        column = (start - start % 2) * PLANE
        blocks.append(ref[kind, comp, start % 2, :, column : column + SITES])
    return jnp.concatenate(blocks, axis=0)


def wave_tables(length):
    ids = np.arange(length)
    angles = (ids[:, None] * ids[None, :] % length) * (2.0 * math.pi / length)
    return np.stack([np.cos(angles), np.sin(angles)]).astype(np.float32)


def last_transform(length):
    cos, sin = wave_tables(length)
    whole = np.concatenate(
        [np.concatenate([cos, -sin], axis=1), np.concatenate([-sin, -cos], axis=1)], axis=0
    )
    return whole.astype(ml_dtypes.bfloat16)


def split(value):
    high = value.astype(BF16)
    return high, (value - high.astype(F32)).astype(BF16)


def quotient(value, by):
    if by & (by - 1) == 0:
        return lax.shift_right_logical(value, int(math.log2(by)))
    return value // by


def remainder(value, by):
    if by & (by - 1) == 0:
        return value & (by - 1)
    return value % by


def dot_nt(left, right):
    return lax.dot_general(left, right, (((1,), (1,)), ((), ())), preferred_element_type=F32)


def dot_tn(left, right):
    return lax.dot_general(left, right, (((0,), (0,)), ((), ())), preferred_element_type=F32)


def dot(left, right):
    return jnp.dot(left, right, preferred_element_type=F32)


def in_hbm(arrays):
    return [pltpu.with_memory_space_constraint(jnp.asarray(a), pltpu.HBM) for a in arrays]


def pack_kernel(cols, tiles_ref, noise_ref, offsets_ref, cells_ref, slot_ref, out_ref):
    units = out_ref.shape[0]
    slots = tiles_ref.shape[3]
    my_row, my_col = lax.axis_index("row"), lax.axis_index("col")
    lane = lax.broadcasted_iota(jnp.int32, (1, TB), 1)
    tiles = jnp.full((1, TB), -1, jnp.int32)
    for slot in range(slots):
        tile_row = tiles_ref[0, 0, 0:1, slot : slot + 1]
        tile_col = tiles_ref[0, 0, 1:2, slot : slot + 1]
        active = tile_row >= 0
        row_unit = jnp.where(active, my_row * cols + tile_row, -1)
        col_unit = jnp.where(active, tile_col * cols + my_col, -1)
        tiles = jnp.where(lane == slot, row_unit, tiles)
        tiles = jnp.where(lane == slot + TB // 2, col_unit, tiles)
    cells = cells_ref[0, 0].astype(F32)
    caps, peers = cells.shape
    if peers < TB:
        cells = jnp.concatenate([cells, jnp.zeros((caps, TB - peers), F32)], axis=1)
        cells = pltpu.roll(cells, 0, 1, stride=peers, stride_axis=0)
        per_row = TB // peers
        cells = jnp.concatenate(
            [
                jnp.sum(cells[at : at + per_row], axis=0, keepdims=True)
                for at in range(0, caps, per_row)
            ],
            axis=0,
        )
    cells = cells.astype(jnp.int32)
    head = [offsets_ref[...], slot_ref[...], tiles]
    head += [quotient(cells, 2 * HALF), remainder(cells, 2 * HALF) - HALF]
    block = jnp.concatenate(
        [noise_ref[0], noise_ref[1], noise_ref[2]] + [part.astype(F32) for part in head], axis=0
    )
    spare = out_ref.shape[1] - block.shape[0]
    if spare:
        block = jnp.concatenate([block, jnp.zeros((spare, TB), F32)], axis=0)
    block = block.astype(BF16)
    for unit in range(units):
        out_ref[unit] = block


def cell_rows(caps, peers):
    per_row = max(1, TB // peers)
    return per_row, -(-caps // per_row)


def pack(noise_field, offsets, tile_list, send_cells, bead_slot, units, cols):
    _, lists = cell_rows(*send_cells.shape[2:])
    rows = -(-(CELLS + 2 * lists) // 16) * 16
    vmem = pl.BlockSpec(memory_space=pltpu.VMEM)
    return pl.pallas_call(
        functools.partial(pack_kernel, cols),
        out_shape=jax.ShapeDtypeStruct((units, rows, TB), BF16),
        in_specs=[vmem] * 5,
        out_specs=vmem,
        name="pack_inputs",
    )(tile_list, noise_field, offsets, send_cells, bead_slot.reshape(1, TB))


def signed(ids, length):
    return jnp.where(ids < length // 2, ids, ids - length).astype(F32)


def spectrum_kernel(
    rows_x, spec_hbm, turn_hbm, wave_hbm, out_ref, phase_ref, spec_ref, turn_ref, wave_ref, sems
):
    steps, _, comps, vecs, part_x, rows_y, length = spec_ref.shape
    depth = part_x * rows_y
    shape = (part_x, rows_y, length)
    copies = [
        pltpu.make_async_copy(
            spec_hbm.at[:, :, :, pl.ds(step * part_x, part_x)], spec_ref.at[step], sems.at[step]
        )
        for step in range(steps)
    ]
    tables = [
        pltpu.make_async_copy(source, target, sems.at[steps + at])
        for at, (source, target) in enumerate(
            [(turn_hbm, turn_ref), (wave_hbm, wave_ref)]
        )
    ]
    copies[0].start()
    tables[0].start()
    for copy in copies[1:] + tables[1:]:
        copy.start()
    wave_y = signed(lax.axis_index("col") * rows_y + lax.broadcasted_iota(jnp.int32, shape, 1), length)
    wave_z = signed(lax.broadcasted_iota(jnp.int32, shape, 2), length)
    width_sq = (length / 8.0) ** 2
    height = math.sqrt(1.5) / (2.0 * math.pi * width_sq) ** 0.75
    for step in range(steps):
        first_x = lax.axis_index("row") * rows_x + step * part_x
        wave_x = signed(first_x + lax.broadcasted_iota(jnp.int32, shape, 0), length)
        wave = (wave_x, wave_y, wave_z)
        wave_sq = wave_x * wave_x + wave_y * wave_y + wave_z * wave_z
        amplitude = height * jnp.exp(wave_sq * (-0.25 / width_sq))
        amplitude = jnp.where(wave_sq > 0, amplitude, 0.0)
        damped = amplitude / jnp.maximum(wave_sq, 1.0)
        copies[step].wait()
        if step == 0:
            tables[0].wait()
        for vec in range(vecs):
            hat = []
            for part in range(2):
                source = [spec_ref[step, part, comp, vec] for comp in range(comps)]
                along = wave_x * source[0] + wave_y * source[1] + wave_z * source[2]
                factor = along * damped
                hat.append(
                    [
                        (amplitude * source[comp] - wave[comp] * factor)
                        .astype(BF16)
                        .reshape(depth, length)
                        for comp in range(comps)
                    ]
                )
            for comp in range(comps):
                both = jnp.concatenate([hat[0][comp], hat[1][comp]], axis=1)
                turned = dot_nt(turn_ref[...], both).astype(BF16)
                at = (comp * vecs + vec) * length
                column = 2 * step * depth
                out_ref[at : at + length, column : column + depth] = turned[:length]
                column += depth
                out_ref[at : at + length, column : column + depth] = turned[length:]
    for table in tables[1:]:
        table.wait()
    for axis, count in enumerate((rows_x, rows_y)):
        first = pl.multiple_of(lax.axis_index(UNIT_AXES[axis]) * count, count)
        parts = [split(wave_ref[part, pl.ds(first, count), :]) for part in range(2)]
        parts = [piece for pair in parts for piece in pair]
        phase_ref[axis, 0 : 4 * count, :] = jnp.concatenate(parts, axis=0)


def chunk_of(rows_x, rows_y):
    part_x = max(1, min(rows_x, 256 // rows_y))
    while rows_x % part_x:
        part_x -= 1
    return part_x


def spectrum(spectral):
    _, comps, vecs, rows_x, rows_y, length = spectral.shape
    part_x = chunk_of(rows_x, rows_y)
    steps = rows_x // part_x
    fields = comps * vecs * length
    sources = [spectral, last_transform(length), wave_tables(length)]
    hbm = pl.BlockSpec(memory_space=pltpu.HBM)
    vmem = pl.BlockSpec(memory_space=pltpu.VMEM)
    return pl.pallas_call(
        functools.partial(spectrum_kernel, rows_x),
        out_shape=[
            pltpu.VMEM((fields, 2 * rows_x * rows_y), BF16),
            pltpu.VMEM((2, 4 * max(rows_x, rows_y), length), BF16),
        ],
        in_specs=[hbm] * 3,
        out_specs=[vmem] * 2,
        scratch_shapes=[
            pltpu.VMEM((steps, 2, comps, vecs, part_x, rows_y, length), F32),
            pltpu.VMEM((2 * length, 2 * length), BF16),
            pltpu.VMEM((2, length, length), F32),
            pltpu.SemaphoreType.DMA((steps + 2,)),
        ],
        compiler_params=pltpu.CompilerParams(vmem_limit_bytes=SPECTRUM_BYTES),
        cost_estimate=pl.CostEstimate(
            flops=2 * 2 * fields * rows_x * rows_y * 2 * length,
            bytes_accessed=spectral.size * 4 + 4 * fields * rows_x * rows_y,
            transcendentals=rows_x * rows_y * length,
        ),
        name="spectrum",
    )(*in_hbm(sources))


def find_cells(cols, slabs, per_row, lists, packed_ref, first, group):
    units = packed_ref.shape[0]
    entries = units * lists
    packed = packed_ref[...].astype(F32)
    high = packed[:, CELLS : CELLS + lists, :].reshape(entries, TB)
    low = packed[:, CELLS + lists : CELLS + 2 * lists, :].reshape(entries, TB)
    cells = (high * (2 * HALF) + (low + HALF)).astype(jnp.int32)
    entry = lax.broadcasted_iota(jnp.int32, cells.shape, 0)
    holder = quotient(entry, lists)
    holder_row = quotient(holder, cols)
    holder_col = holder - holder_row * cols
    rest = quotient(cells, slabs[1])
    digits = [
        quotient(rest, slabs[0]),
        holder_row * slabs[0] + remainder(rest, slabs[0]),
        holder_col * slabs[1] + remainder(cells, slabs[1]),
    ]
    digits = jnp.concatenate([d.astype(F32).astype(BF16) for d in digits], axis=1)
    beads = group * TB
    slot = jnp.concatenate(
        [packed_ref[first + unit].astype(F32)[SLOT : SLOT + 1] for unit in range(group)], axis=1
    ).astype(jnp.int32)
    owner = first + quotient(lax.broadcasted_iota(jnp.int32, (1, beads), 1), TB)
    order = quotient(slot, units)
    index = remainder(slot, units) * lists + quotient(order, per_row)
    lane = remainder(order, per_row) * units + owner
    chosen = lax.broadcasted_iota(jnp.int32, (entries, beads), 0) == index
    found = dot_tn(digits, jnp.where(chosen, 1.0, 0.0).astype(BF16))
    mine = lax.broadcasted_iota(jnp.int32, (TB, beads), 0) == lane
    return [
        jnp.sum(
            jnp.where(mine, found[digit * TB : (digit + 1) * TB], 0.0), axis=0, keepdims=True
        ).astype(jnp.int32)
        for digit in range(3)
    ]


def sample_kernel(
    cols, slabs, rows, lists, groups, packed_ref, field_ref, table_ref, out_ref, *phase_refs
):
    length = table_ref.shape[2]
    comps, vecs = out_ref.shape[1:3]
    rows_y = rows[1]
    part_x = chunk_of(*rows)
    depth = 2 * part_x * rows_y

    def hits(place):
        position = lax.broadcasted_iota(jnp.int32, (length, place.shape[1]), 0)
        return position == place

    def phases(axis, place):
        count = rows[axis]
        found = dot(table_ref[axis, 0 : 4 * count, :], jnp.where(hits(place), 1.0, 0.0).astype(BF16))
        found = [found[at * count : (at + 1) * count] for at in range(4)]
        return found[0] + found[1], found[2] + found[3]

    def fill(first, group, phase_ref):
        first = pl.program_id(0) * out_ref.shape[0] + first
        beads = group * TB
        place = find_cells(cols, slabs, lists[0], lists[1], packed_ref, first, group)
        cos_x, sin_x = phases(0, place[0])
        cos_y, sin_y = [v.astype(BF16) for v in phases(1, place[1])]
        for x in range(rows[0]):
            cos_one = jnp.broadcast_to(cos_x[x : x + 1], (rows_y, beads)).astype(BF16)
            sin_one = jnp.broadcast_to(sin_x[x : x + 1], (rows_y, beads)).astype(BF16)
            at = x // part_x * depth + x % part_x * rows_y
            phase_ref[at : at + rows_y, :] = cos_one * cos_y - sin_one * sin_y
            at += depth // 2
            phase_ref[at : at + rows_y, :] = cos_one * sin_y + sin_one * cos_y
        return place[2]

    def finish(first, group, total, place_z):
        chosen = hits(place_z)
        for comp in range(comps):
            for vec in range(vecs):
                at = (comp * vecs + vec) * length
                picked = jnp.where(chosen, total[at : at + length], 0.0)
                picked = jnp.sum(picked, axis=0, keepdims=True)
                for unit in range(group):
                    out_ref[first + unit, comp, vec : vec + 1, :] = picked[
                        :, unit * TB : (unit + 1) * TB
                    ]

    starts = [sum(groups[:at]) for at in range(len(groups))]
    place_z = fill(0, groups[0], phase_refs[0])
    for at, group in enumerate(groups):
        later = None
        if at + 1 < len(groups):
            later = fill(starts[at + 1], groups[at + 1], phase_refs[at + 1])
        total = dot(field_ref[...], phase_refs[at][...])
        finish(starts[at], group, total, place_z)
        place_z = later


def sample(packed, field, table, spectral_shape, cells_shape, rows, cols):
    _, comps, vecs, rows_x, rows_y, length = spectral_shape
    units = rows * cols
    groups = (2, 6, 8) if units % 16 == 0 else (units,)
    whole = sum(groups)
    depth = rows_x * rows_y
    count = comps * vecs
    slabs = (length // rows, length // cols)
    lists = cell_rows(*cells_shape[2:])
    vmem = pl.BlockSpec(memory_space=pltpu.VMEM)
    return pl.pallas_call(
        functools.partial(sample_kernel, cols, slabs, (rows_x, rows_y), lists, groups),
        grid=(units // whole,),
        out_shape=jax.ShapeDtypeStruct((units, comps, vecs, TB), F32),
        in_specs=[vmem] * 3,
        out_specs=pl.BlockSpec((whole, comps, vecs, TB), lambda i: (i, 0, 0, 0)),
        scratch_shapes=[pltpu.VMEM((2 * depth, group * TB), BF16) for group in groups],
        compiler_params=pltpu.CompilerParams(vmem_limit_bytes=SAMPLE_BYTES),
        cost_estimate=pl.CostEstimate(
            flops=2 * 2 * depth * count * length * units * TB,
            bytes_accessed=field.size * 2,
            transcendentals=0,
        ),
        name="sample_far",
    )(packed, field, table)


def over(count, term, sum_refs):
    if not sum_refs:
        return functools.reduce(lambda a, b: a + b, [term(at) for at in range(count)])
    sum_ref = sum_refs[0]
    sum_ref[...] = term(0)

    def step(at, carry):
        sum_ref[...] += term(at)
        return carry

    lax.fori_loop(1, count, step, 0)
    return sum_ref[...]


def near_kernel(
    units, cols, slots, vecs, packed_ref, noise_ref, table_hbm, energy_hbm, half_hbm, out_ref,
    table_ref, energy_ref, half_ref, rows_ref, sems, *sum_refs,
):
    copies = [
        pltpu.make_async_copy(table_hbm, table_ref, sems.at[0]),
        pltpu.make_async_copy(energy_hbm, energy_ref, sems.at[1]),
        pltpu.make_async_copy(half_hbm, half_ref, sems.at[2]),
    ]
    for copy in copies:
        copy.start()

    part = vecs * units
    wide = 4 * part
    fields = 3 * vecs
    group = min(units, 16)
    site = lax.broadcasted_iota(jnp.int32, (SITES, TB), 0)
    block_of = quotient(lax.broadcasted_iota(jnp.int32, (SITES, wide), 1), part)

    def sites_of(unit):
        rows = packed_ref[unit].astype(F32)[OFFSETS : OFFSETS + 3]
        code = (rows[0:1] * PERIOD + rows[1:2]) * PERIOD + rows[2:3]
        return jnp.where(site == code.astype(jnp.int32), 1.0, 0.0).astype(BF16)

    def scatter(first):
        held, spread = [], []
        for at in range(group):
            unit = first + at
            held.append(sites_of(unit))
            noise = packed_ref[unit].astype(F32)[0:fields]
            pieces = jnp.concatenate([noise, jnp.ones((vecs, TB), F32)], axis=0)
            mine = lax.broadcasted_iota(jnp.int32, (4 * vecs, units, TB), 1) == unit
            block = jnp.where(mine, pieces[:, None, :], 0.0)
            spread.append(block.reshape(wide, TB).astype(BF16))
        return dot_nt(jnp.concatenate(held, axis=1), jnp.concatenate(spread, axis=1))

    lattice = over(units // group, lambda at: scatter(at * group), sum_refs[:1])
    to_all = lax.broadcasted_iota(jnp.int32, (wide, wide), 0) == 3 * part + remainder(
        lax.broadcasted_iota(jnp.int32, (wide, wide), 1), units
    )
    count = dot(lattice.astype(BF16), jnp.where(to_all, 1.0, 0.0).astype(BF16))

    lane = lax.broadcasted_iota(jnp.int32, (units, wide), 1)
    tiles = packed_ref[...].astype(F32)[:, TILES, :].astype(jnp.int32)
    tile_lane = lax.broadcasted_iota(jnp.int32, (units, TB), 1)

    def links(slot):
        row_unit, col_unit = [
            jnp.sum(jnp.where(tile_lane == slot + start, tiles, 0), axis=1, keepdims=True)
            for start in (0, TB // 2)
        ]
        active = row_unit >= 0
        from_col, to_row = [], []
        for vec in range(vecs):
            for comp in range(3):

                def hot(unit, at):
                    hit = active & (lane == unit + (at * part + vec * units))
                    return jnp.where(hit, 1.0, 0.0)

                from_col.append(hot(col_unit, comp))
                to_row.append(
                    jnp.concatenate([hot(row_unit, (comp - turn) % 3) for turn in range(3)], axis=1)
                )
        from_col = jnp.concatenate(from_col, axis=0).astype(BF16)
        return dot_tn(from_col, jnp.concatenate(to_row, axis=0).astype(BF16))

    mix = over(slots, links, sum_refs[1:])
    mix = mix.astype(BF16)
    mix = jnp.concatenate([mix, mix], axis=0)

    def in_block(block, value):
        return jnp.where(block_of == block, value, 0.0)

    def in_half_block(block, value):
        return jnp.where(block_of[:HALVED] == block, value, 0.0)

    for copy in copies[:2]:
        copy.wait()

    halves = [jnp.concatenate([half.astype(BF16)] * 2, axis=0) for half in halve(count)]
    energy = None
    for comp in range(3):
        plus, minus = [dot(energy_ref[comp, kind], half) for kind, half in enumerate(halves)]
        term = in_block(comp, unhalve(plus, minus))
        energy = term if energy is None else energy + term
    energy = dot(jnp.concatenate(split(energy), axis=1), mix[:, :wide])
    occupied = (count > 0.5) & (block_of < 3)
    largest = jnp.max(jnp.where(occupied, energy, 0.0), keepdims=True)
    scaling = lax.rsqrt(largest + 1e-06)

    def product(vector):
        mixed = dot(jnp.concatenate(split(vector), axis=1), mix).astype(BF16)
        result = None
        for comp in range(3):
            same = dot(whole_table(table_ref, 0, comp), mixed[:, :wide])
            other = dot(whole_table(table_ref, 1, comp), mixed[:, wide:])
            term = in_block(comp, same + other[:, :wide]) + in_block(
                (comp + 1) % 3, other[:, wide:]
            )
            result = term if result is None else result + term
        return result

    def halved_product(vector):
        mixed = dot(jnp.concatenate(split(jnp.concatenate(halve(vector), axis=0)), axis=1), mix).astype(BF16)
        results = []
        for kind in range(2):
            half = mixed[kind * HALVED : (kind + 1) * HALVED]
            same = dot(half_ref[0, kind], half[:, :wide])
            other = dot(half_ref[1, kind], half[:, wide:])
            result = None
            for comp in range(3):
                rows = slice(comp * HALVED, (comp + 1) * HALVED)
                term = in_half_block(comp, same[rows] + other[rows, :wide])
                term = term + in_half_block((comp + 1) % 3, other[rows, wide:])
                result = term if result is None else result + term
            results.append(result)
        return unhalve(*results)

    weights = (
        cheb_coef[1] - cheb_coef[3],
        2.0 * (cheb_coef[2] - cheb_coef[4]),
        2.0 * cheb_coef[3],
        2.0 * cheb_coef[4],
    )
    weight = count * scaling
    previous, current, total = None, lattice, None
    for degree in range(4):
        if degree == 1:
            copies[2].wait()
        result = product(current) if degree < 1 else halved_product(current)
        scaled = weights[degree] * result
        total = scaled if total is None else total + scaled
        if degree < 3:
            following = weight * result
            if previous is not None:
                following = 2.0 * following - previous
            previous, current = current, following

    me = lax.axis_index("row") * cols + lax.axis_index("col")
    high, low = split(total)
    held = sites_of(me)
    rows_ref[...] = dot_tn(high, held) + dot_tn(low, held)
    first_weight = cheb_coef[0] - cheb_coef[2] + cheb_coef[4]
    for comp in range(3):
        for vec in range(vecs):
            near = rows_ref[pl.ds(comp * part + vec * units + me, 1), :] * scaling
            out_ref[comp, vec : vec + 1, :] = first_weight * noise_ref[comp, vec : vec + 1, :] + near


def near(packed, noise_field, units, cols, slots):
    vecs = noise_field.shape[1]
    wide = 4 * vecs * units
    tables = kernel_tables()
    vmem = pl.BlockSpec(memory_space=pltpu.VMEM)
    hbm = pl.BlockSpec(memory_space=pltpu.HBM)
    sums = [(SITES, wide), (wide, 3 * wide)] if units > 16 else []
    return pl.pallas_call(
        functools.partial(near_kernel, units, cols, slots, vecs),
        out_shape=pltpu.VMEM((3, vecs, TB), F32),
        in_specs=[vmem] * 2 + [hbm] * 3,
        out_specs=vmem,
        scratch_shapes=[pltpu.VMEM(table.shape, BF16) for table in tables]
        + [pltpu.VMEM((wide, TB), F32), pltpu.SemaphoreType.DMA((3,))]
        + [pltpu.VMEM(shape, F32) for shape in sums],
        compiler_params=pltpu.CompilerParams(vmem_limit_bytes=NEAR_BYTES),
        cost_estimate=pl.CostEstimate(
            flops=4 * 2 * 9 * SITES * SITES * 256, bytes_accessed=8 * 10**6, transcendentals=0
        ),
        name="near_field",
    )(packed, noise_field, *in_hbm(tables))


def per_device(noise_field, offsets, tile_list, send_cells, bead_slot, spectral):
    rows, cols = lax.axis_size("row"), lax.axis_size("col")
    units = rows * cols

    def exchange(blocks):
        return lax.all_to_all(blocks, UNIT_AXES, split_axis=0, concat_axis=0, tiled=True)

    packed = exchange(
        pack(noise_field, offsets, tile_list, send_cells, bead_slot, units, cols)
    )
    field, waves = spectrum(spectral)
    far = sample(packed, field, waves, spectral.shape, send_cells.shape, rows, cols)
    partial = exchange(far)
    near_field = near(packed, noise_field, units, cols, tile_list.shape[3])
    return near_field + jnp.sum(partial, axis=0)


def solution(mesh):
    return jax.shard_map(
        per_device,
        mesh=mesh,
        in_specs=(
            P(None, None, ("groups", "row", "col")),
            P(None, ("groups", "row", "col")),
            P(("groups", "row"), "col", None, None),
            P(("groups", "row"), "col", None, None),
            P(("groups", "row", "col")),
            P(None, None, None, ("groups", "row"), "col", None),
        ),
        out_specs=P(None, None, ("groups", "row", "col")),
        check_vma=False,
    )
```

```python
import functools
import math

import jax
import jax.numpy as jnp
import ml_dtypes
import numpy as np
from jax import lax
from jax.experimental import pallas as pl
from jax.experimental.pallas import tpu as pltpu
from jax.sharding import PartitionSpec as P

TB = 128
PERIOD = 8
SITES = PERIOD**3
PLANE = PERIOD**2
WINDOW = SITES + (PERIOD - 2) * PLANE
HALVED = SITES // 2
OFFSETS, SLOT, TILES, CELLS = 6, 9, 10, 11
HALF = 256
UNIT_AXES = ("row", "col")
MIB = 1024 * 1024
SPECTRUM_BYTES, SAMPLE_BYTES, NEAR_BYTES = 28 * MIB, 28 * MIB, 50 * MIB

cheb_coef = (1.0, 0.45, -0.2, 0.12, -0.08)
kernel_range = 1.5

F32 = jnp.float32
BF16 = jnp.bfloat16


def kernel_tables():
    ids = np.arange(SITES)
    coords = np.stack([ids // PERIOD**2, ids // PERIOD % PERIOD, ids % PERIOD])
    half = PERIOD // 2
    displace = (coords[:, :, None] - coords[:, None, :] + half) % PERIOD - half
    displace = displace.astype(np.float32)
    squares = (displace * displace).sum(0)
    scale_sq = np.float32(kernel_range * kernel_range)
    envelope = np.exp(squares * np.float32(-0.5 / scale_sq)) / scale_sq
    same, other = [], []
    for left in range(3):
        right = (left + 1) % 3
        same.append(envelope * (displace[left] * displace[left] - squares / np.float32(3.0)))
        other.append(envelope * (displace[left] * displace[right]))
    same = np.stack(same).astype(ml_dtypes.bfloat16)
    other = np.stack(other).astype(ml_dtypes.bfloat16)
    squared = [np.square(t.astype(np.float32)) for t in (same, other)]
    energy = squared[0] + squared[1] + np.roll(squared[1], 1, axis=0)
    columns = (np.arange(WINDOW)[None, :] + np.array([[0], [PLANE]])) % SITES
    rows = np.stack([same, other])[:, :, :PLANE]
    windows = np.stack([rows[..., shifted] for shifted in columns], axis=2)
    energy_halves = halved_tables(energy)
    pair_halves = halved_tables(np.stack([same, other]).astype(np.float32))[0]
    pair_halves = np.moveaxis(pair_halves, 2, 1).reshape(2, 2, 3 * HALVED, HALVED)
    return windows, np.concatenate(energy_halves, axis=3), pair_halves


def halved_tables(tables):
    first, last = tables[..., :HALVED, :HALVED], tables[..., :HALVED, HALVED:]
    halves = 0.5 * np.stack([first + last, first - last], axis=-3)
    high = halves.astype(ml_dtypes.bfloat16)
    return high, (halves - high.astype(np.float32)).astype(ml_dtypes.bfloat16)


def halve(value):
    return value[:HALVED] + value[HALVED:], value[:HALVED] - value[HALVED:]


def unhalve(plus, minus):
    return jnp.concatenate([plus + minus, plus - minus], axis=0)


def whole_table(ref, kind, comp):
    blocks = []
    for first in range(PERIOD):
        start = -first % PERIOD
        column = (start - start % 2) * PLANE
        blocks.append(ref[kind, comp, start % 2, :, column : column + SITES])
    return jnp.concatenate(blocks, axis=0)


def wave_tables(length):
    ids = np.arange(length)
    angles = (ids[:, None] * ids[None, :] % length) * (2.0 * math.pi / length)
    return np.stack([np.cos(angles), np.sin(angles)]).astype(np.float32)


def last_transform(length):
    cos, sin = wave_tables(length)
    whole = np.concatenate(
        [np.concatenate([cos, -sin], axis=1), np.concatenate([-sin, -cos], axis=1)], axis=0
    )
    return whole.astype(ml_dtypes.bfloat16)


def split(value):
    high = value.astype(BF16)
    return high, (value - high.astype(F32)).astype(BF16)


def quotient(value, by):
    if by & (by - 1) == 0:
        return lax.shift_right_logical(value, int(math.log2(by)))
    return value // by


def remainder(value, by):
    if by & (by - 1) == 0:
        return value & (by - 1)
    return value % by


def dot_nt(left, right):
    return lax.dot_general(left, right, (((1,), (1,)), ((), ())), preferred_element_type=F32)


def dot_tn(left, right):
    return lax.dot_general(left, right, (((0,), (0,)), ((), ())), preferred_element_type=F32)


def dot(left, right):
    return jnp.dot(left, right, preferred_element_type=F32)


def in_hbm(arrays):
    return [pltpu.with_memory_space_constraint(jnp.asarray(a), pltpu.HBM) for a in arrays]


def pack_kernel(cols, tiles_ref, noise_ref, offsets_ref, cells_ref, slot_ref, out_ref):
    units = out_ref.shape[0]
    slots = tiles_ref.shape[3]
    my_row, my_col = lax.axis_index("row"), lax.axis_index("col")
    lane = lax.broadcasted_iota(jnp.int32, (1, TB), 1)
    tiles = jnp.full((1, TB), -1, jnp.int32)
    for slot in range(slots):
        tile_row = tiles_ref[0, 0, 0:1, slot : slot + 1]
        tile_col = tiles_ref[0, 0, 1:2, slot : slot + 1]
        active = tile_row >= 0
        row_unit = jnp.where(active, my_row * cols + tile_row, -1)
        col_unit = jnp.where(active, tile_col * cols + my_col, -1)
        tiles = jnp.where(lane == slot, row_unit, tiles)
        tiles = jnp.where(lane == slot + TB // 2, col_unit, tiles)
    cells = cells_ref[0, 0].astype(F32)
    caps, peers = cells.shape
    if peers < TB:
        cells = jnp.concatenate([cells, jnp.zeros((caps, TB - peers), F32)], axis=1)
        cells = pltpu.roll(cells, 0, 1, stride=peers, stride_axis=0)
        per_row = TB // peers
        cells = jnp.concatenate(
            [
                jnp.sum(cells[at : at + per_row], axis=0, keepdims=True)
                for at in range(0, caps, per_row)
            ],
            axis=0,
        )
    cells = cells.astype(jnp.int32)
    head = [offsets_ref[...], slot_ref[...], tiles]
    head += [quotient(cells, 2 * HALF), remainder(cells, 2 * HALF) - HALF]
    block = jnp.concatenate(
        [noise_ref[0], noise_ref[1], noise_ref[2]] + [part.astype(F32) for part in head], axis=0
    )
    spare = out_ref.shape[1] - block.shape[0]
    if spare:
        block = jnp.concatenate([block, jnp.zeros((spare, TB), F32)], axis=0)
    block = block.astype(BF16)
    for unit in range(units):
        out_ref[unit] = block


def cell_rows(caps, peers):
    per_row = max(1, TB // peers)
    return per_row, -(-caps // per_row)


def pack(noise_field, offsets, tile_list, send_cells, bead_slot, units, cols):
    _, lists = cell_rows(*send_cells.shape[2:])
    rows = -(-(CELLS + 2 * lists) // 16) * 16
    vmem = pl.BlockSpec(memory_space=pltpu.VMEM)
    return pl.pallas_call(
        functools.partial(pack_kernel, cols),
        out_shape=jax.ShapeDtypeStruct((units, rows, TB), BF16),
        in_specs=[vmem] * 5,
        out_specs=vmem,
        name="pack_inputs",
    )(tile_list, noise_field, offsets, send_cells, bead_slot.reshape(1, TB))


def signed(ids, length):
    return jnp.where(ids < length // 2, ids, ids - length).astype(F32)


def spectrum_kernel(
    rows_x, spec_hbm, turn_hbm, wave_hbm, out_ref, phase_ref, spec_ref, turn_ref, wave_ref, sems
):
    steps, _, comps, vecs, part_x, rows_y, length = spec_ref.shape
    depth = part_x * rows_y
    shape = (part_x, rows_y, length)
    copies = [
        pltpu.make_async_copy(
            spec_hbm.at[:, :, :, pl.ds(step * part_x, part_x)], spec_ref.at[step], sems.at[step]
        )
        for step in range(steps)
    ]
    tables = [
        pltpu.make_async_copy(source, target, sems.at[steps + at])
        for at, (source, target) in enumerate(
            [(turn_hbm, turn_ref), (wave_hbm, wave_ref)]
        )
    ]
    copies[0].start()
    tables[0].start()
    for copy in copies[1:] + tables[1:]:
        copy.start()
    wave_y = signed(lax.axis_index("col") * rows_y + lax.broadcasted_iota(jnp.int32, shape, 1), length)
    wave_z = signed(lax.broadcasted_iota(jnp.int32, shape, 2), length)
    width_sq = (length / 8.0) ** 2
    height = math.sqrt(1.5) / (2.0 * math.pi * width_sq) ** 0.75
    for step in range(steps):
        first_x = lax.axis_index("row") * rows_x + step * part_x
        wave_x = signed(first_x + lax.broadcasted_iota(jnp.int32, shape, 0), length)
        wave = (wave_x, wave_y, wave_z)
        wave_sq = wave_x * wave_x + wave_y * wave_y + wave_z * wave_z
        amplitude = height * jnp.exp(wave_sq * (-0.25 / width_sq))
        amplitude = jnp.where(wave_sq > 0, amplitude, 0.0)
        damped = amplitude / jnp.maximum(wave_sq, 1.0)
        copies[step].wait()
        if step == 0:
            tables[0].wait()
        for vec in range(vecs):
            hat = []
            for part in range(2):
                source = [spec_ref[step, part, comp, vec] for comp in range(comps)]
                along = wave_x * source[0] + wave_y * source[1] + wave_z * source[2]
                factor = along * damped
                hat.append(
                    [
                        (amplitude * source[comp] - wave[comp] * factor)
                        .astype(BF16)
                        .reshape(depth, length)
                        for comp in range(comps)
                    ]
                )
            for comp in range(comps):
                both = jnp.concatenate([hat[0][comp], hat[1][comp]], axis=1)
                turned = dot_nt(turn_ref[...], both).astype(BF16)
                at = (comp * vecs + vec) * length
                column = 2 * step * depth
                out_ref[at : at + length, column : column + depth] = turned[:length]
                column += depth
                out_ref[at : at + length, column : column + depth] = turned[length:]
    for table in tables[1:]:
        table.wait()
    for axis, count in enumerate((rows_x, rows_y)):
        first = pl.multiple_of(lax.axis_index(UNIT_AXES[axis]) * count, count)
        parts = [split(wave_ref[part, pl.ds(first, count), :]) for part in range(2)]
        parts = [piece for pair in parts for piece in pair]
        phase_ref[axis, 0 : 4 * count, :] = jnp.concatenate(parts, axis=0)


def chunk_of(rows_x, rows_y):
    part_x = max(1, min(rows_x, 256 // rows_y))
    while rows_x % part_x:
        part_x -= 1
    return part_x


def spectrum(spectral):
    _, comps, vecs, rows_x, rows_y, length = spectral.shape
    part_x = chunk_of(rows_x, rows_y)
    steps = rows_x // part_x
    fields = comps * vecs * length
    sources = [spectral, last_transform(length), wave_tables(length)]
    hbm = pl.BlockSpec(memory_space=pltpu.HBM)
    vmem = pl.BlockSpec(memory_space=pltpu.VMEM)
    return pl.pallas_call(
        functools.partial(spectrum_kernel, rows_x),
        out_shape=[
            pltpu.VMEM((fields, 2 * rows_x * rows_y), BF16),
            pltpu.VMEM((2, 4 * max(rows_x, rows_y), length), BF16),
        ],
        in_specs=[hbm] * 3,
        out_specs=[vmem] * 2,
        scratch_shapes=[
            pltpu.VMEM((steps, 2, comps, vecs, part_x, rows_y, length), F32),
            pltpu.VMEM((2 * length, 2 * length), BF16),
            pltpu.VMEM((2, length, length), F32),
            pltpu.SemaphoreType.DMA((steps + 2,)),
        ],
        compiler_params=pltpu.CompilerParams(vmem_limit_bytes=SPECTRUM_BYTES),
        cost_estimate=pl.CostEstimate(
            flops=2 * 2 * fields * rows_x * rows_y * 2 * length,
            bytes_accessed=spectral.size * 4 + 4 * fields * rows_x * rows_y,
            transcendentals=rows_x * rows_y * length,
        ),
        name="spectrum",
    )(*in_hbm(sources))


def find_cells(cols, slabs, per_row, lists, packed_ref, first, group):
    units = packed_ref.shape[0]
    entries = units * lists
    packed = packed_ref[...].astype(F32)
    high = packed[:, CELLS : CELLS + lists, :].reshape(entries, TB)
    low = packed[:, CELLS + lists : CELLS + 2 * lists, :].reshape(entries, TB)
    cells = (high * (2 * HALF) + (low + HALF)).astype(jnp.int32)
    entry = lax.broadcasted_iota(jnp.int32, cells.shape, 0)
    holder = quotient(entry, lists)
    holder_row = quotient(holder, cols)
    holder_col = holder - holder_row * cols
    rest = quotient(cells, slabs[1])
    digits = [
        quotient(rest, slabs[0]),
        holder_row * slabs[0] + remainder(rest, slabs[0]),
        holder_col * slabs[1] + remainder(cells, slabs[1]),
    ]
    digits = jnp.concatenate([d.astype(F32).astype(BF16) for d in digits], axis=1)
    beads = group * TB
    slot = jnp.concatenate(
        [packed_ref[first + unit].astype(F32)[SLOT : SLOT + 1] for unit in range(group)], axis=1
    ).astype(jnp.int32)
    owner = first + quotient(lax.broadcasted_iota(jnp.int32, (1, beads), 1), TB)
    order = quotient(slot, units)
    index = remainder(slot, units) * lists + quotient(order, per_row)
    lane = remainder(order, per_row) * units + owner
    chosen = lax.broadcasted_iota(jnp.int32, (entries, beads), 0) == index
    found = dot_tn(digits, jnp.where(chosen, 1.0, 0.0).astype(BF16))
    mine = lax.broadcasted_iota(jnp.int32, (TB, beads), 0) == lane
    return [
        jnp.sum(
            jnp.where(mine, found[digit * TB : (digit + 1) * TB], 0.0), axis=0, keepdims=True
        ).astype(jnp.int32)
        for digit in range(3)
    ]


def sample_kernel(
    cols, slabs, rows, lists, groups, packed_ref, field_ref, table_ref, out_ref, *phase_refs
):
    length = table_ref.shape[2]
    comps, vecs = out_ref.shape[1:3]
    rows_y = rows[1]
    part_x = chunk_of(*rows)
    depth = 2 * part_x * rows_y

    def hits(place):
        position = lax.broadcasted_iota(jnp.int32, (length, place.shape[1]), 0)
        return position == place

    def phases(axis, place):
        count = rows[axis]
        found = dot(table_ref[axis, 0 : 4 * count, :], jnp.where(hits(place), 1.0, 0.0).astype(BF16))
        found = [found[at * count : (at + 1) * count] for at in range(4)]
        return found[0] + found[1], found[2] + found[3]

    def fill(first, group, phase_ref):
        first = pl.program_id(0) * out_ref.shape[0] + first
        beads = group * TB
        place = find_cells(cols, slabs, lists[0], lists[1], packed_ref, first, group)
        cos_x, sin_x = phases(0, place[0])
        cos_y, sin_y = [v.astype(BF16) for v in phases(1, place[1])]
        for x in range(rows[0]):
            cos_one = jnp.broadcast_to(cos_x[x : x + 1], (rows_y, beads)).astype(BF16)
            sin_one = jnp.broadcast_to(sin_x[x : x + 1], (rows_y, beads)).astype(BF16)
            at = x // part_x * depth + x % part_x * rows_y
            phase_ref[at : at + rows_y, :] = cos_one * cos_y - sin_one * sin_y
            at += depth // 2
            phase_ref[at : at + rows_y, :] = cos_one * sin_y + sin_one * cos_y
        return place[2]

    def order(unit):
        if out_ref.shape[0] != packed_ref.shape[0]:
            return unit
        return unit % cols * (packed_ref.shape[0] // cols) + unit // cols

    def finish(first, group, total, place_z):
        chosen = hits(place_z)
        for comp in range(comps):
            for vec in range(vecs):
                at = (comp * vecs + vec) * length
                picked = jnp.where(chosen, total[at : at + length], 0.0)
                picked = jnp.sum(picked, axis=0, keepdims=True)
                for unit in range(group):
                    owner = order(first + unit)
                    out_ref[owner, comp, vec : vec + 1, :] = picked[
                        :, unit * TB : (unit + 1) * TB
                    ]

    starts = [sum(groups[:at]) for at in range(len(groups))]
    place_z = fill(0, groups[0], phase_refs[0])
    for at, group in enumerate(groups):
        later = None
        if at + 1 < len(groups):
            later = fill(starts[at + 1], groups[at + 1], phase_refs[at + 1])
        total = dot(field_ref[...], phase_refs[at][...])
        finish(starts[at], group, total, place_z)
        place_z = later


def sample(packed, field, table, spectral_shape, cells_shape, rows, cols):
    _, comps, vecs, rows_x, rows_y, length = spectral_shape
    units = rows * cols
    groups = (2, 6, 8) if units % 16 == 0 else (units,)
    whole = sum(groups)
    depth = rows_x * rows_y
    count = comps * vecs
    slabs = (length // rows, length // cols)
    lists = cell_rows(*cells_shape[2:])
    vmem = pl.BlockSpec(memory_space=pltpu.VMEM)
    return pl.pallas_call(
        functools.partial(sample_kernel, cols, slabs, (rows_x, rows_y), lists, groups),
        grid=(units // whole,),
        out_shape=jax.ShapeDtypeStruct((units, comps, vecs, TB), F32),
        in_specs=[vmem] * 3,
        out_specs=pl.BlockSpec((whole, comps, vecs, TB), lambda i: (i, 0, 0, 0)),
        scratch_shapes=[pltpu.VMEM((2 * depth, group * TB), BF16) for group in groups],
        compiler_params=pltpu.CompilerParams(vmem_limit_bytes=SAMPLE_BYTES),
        cost_estimate=pl.CostEstimate(
            flops=2 * 2 * depth * count * length * units * TB,
            bytes_accessed=field.size * 2,
            transcendentals=0,
        ),
        name="sample_far",
    )(packed, field, table)


def over(count, term, sum_refs):
    if not sum_refs:
        return functools.reduce(lambda a, b: a + b, [term(at) for at in range(count)])
    sum_ref = sum_refs[0]
    sum_ref[...] = term(0)

    def step(at, carry):
        sum_ref[...] += term(at)
        return carry

    lax.fori_loop(1, count, step, 0)
    return sum_ref[...]


def near_kernel(
    units, cols, slots, vecs, packed_ref, noise_ref, table_hbm, energy_hbm, half_hbm, out_ref,
    table_ref, energy_ref, half_ref, rows_ref, sems, *sum_refs,
):
    copies = [
        pltpu.make_async_copy(table_hbm, table_ref, sems.at[0]),
        pltpu.make_async_copy(energy_hbm, energy_ref, sems.at[1]),
        pltpu.make_async_copy(half_hbm, half_ref, sems.at[2]),
    ]
    for copy in copies:
        copy.start()

    part = vecs * units
    wide = 4 * part
    fields = 3 * vecs
    group = min(units, 16)
    site = lax.broadcasted_iota(jnp.int32, (SITES, TB), 0)
    block_of = quotient(lax.broadcasted_iota(jnp.int32, (SITES, wide), 1), part)

    def sites_of(unit):
        rows = packed_ref[unit].astype(F32)[OFFSETS : OFFSETS + 3]
        code = (rows[0:1] * PERIOD + rows[1:2]) * PERIOD + rows[2:3]
        return jnp.where(site == code.astype(jnp.int32), 1.0, 0.0).astype(BF16)

    def scatter(first):
        held, spread = [], []
        for at in range(group):
            unit = first + at
            held.append(sites_of(unit))
            noise = packed_ref[unit].astype(F32)[0:fields]
            pieces = jnp.concatenate([noise, jnp.ones((vecs, TB), F32)], axis=0)
            mine = lax.broadcasted_iota(jnp.int32, (4 * vecs, units, TB), 1) == unit
            block = jnp.where(mine, pieces[:, None, :], 0.0)
            spread.append(block.reshape(wide, TB).astype(BF16))
        return dot_nt(jnp.concatenate(held, axis=1), jnp.concatenate(spread, axis=1))

    lattice = over(units // group, lambda at: scatter(at * group), sum_refs[:1])
    to_all = lax.broadcasted_iota(jnp.int32, (wide, wide), 0) == 3 * part + remainder(
        lax.broadcasted_iota(jnp.int32, (wide, wide), 1), units
    )
    count = dot(lattice.astype(BF16), jnp.where(to_all, 1.0, 0.0).astype(BF16))

    lane = lax.broadcasted_iota(jnp.int32, (units, wide), 1)
    tiles = packed_ref[...].astype(F32)[:, TILES, :].astype(jnp.int32)
    tile_lane = lax.broadcasted_iota(jnp.int32, (units, TB), 1)

    def links(slot):
        row_unit, col_unit = [
            jnp.sum(jnp.where(tile_lane == slot + start, tiles, 0), axis=1, keepdims=True)
            for start in (0, TB // 2)
        ]
        active = row_unit >= 0
        from_col, to_row = [], []
        for vec in range(vecs):
            for comp in range(3):

                def hot(unit, at):
                    hit = active & (lane == unit + (at * part + vec * units))
                    return jnp.where(hit, 1.0, 0.0)

                from_col.append(hot(col_unit, comp))
                to_row.append(
                    jnp.concatenate([hot(row_unit, (comp - turn) % 3) for turn in range(3)], axis=1)
                )
        from_col = jnp.concatenate(from_col, axis=0).astype(BF16)
        return dot_tn(from_col, jnp.concatenate(to_row, axis=0).astype(BF16))

    mix = over(slots, links, sum_refs[1:])
    mix = mix.astype(BF16)
    mix = jnp.concatenate([mix, mix], axis=0)

    def in_block(block, value):
        return jnp.where(block_of == block, value, 0.0)

    def in_half_block(block, value):
        return jnp.where(block_of[:HALVED] == block, value, 0.0)

    for copy in copies[:2]:
        copy.wait()

    halves = [jnp.concatenate([half.astype(BF16)] * 2, axis=0) for half in halve(count)]
    energy = None
    for comp in range(3):
        plus, minus = [dot(energy_ref[comp, kind], half) for kind, half in enumerate(halves)]
        term = in_block(comp, unhalve(plus, minus))
        energy = term if energy is None else energy + term
    energy = dot(jnp.concatenate(split(energy), axis=1), mix[:, :wide])
    occupied = (count > 0.5) & (block_of < 3)
    largest = jnp.max(jnp.where(occupied, energy, 0.0), keepdims=True)
    scaling = lax.rsqrt(largest + 1e-06)

    def product(vector):
        mixed = dot(jnp.concatenate(split(vector), axis=1), mix).astype(BF16)
        result = None
        for comp in range(3):
            same = dot(whole_table(table_ref, 0, comp), mixed[:, :wide])
            other = dot(whole_table(table_ref, 1, comp), mixed[:, wide:])
            term = in_block(comp, same + other[:, :wide]) + in_block(
                (comp + 1) % 3, other[:, wide:]
            )
            result = term if result is None else result + term
        return result

    def halved_product(vector):
        mixed = dot(jnp.concatenate(split(jnp.concatenate(halve(vector), axis=0)), axis=1), mix).astype(BF16)
        results = []
        for kind in range(2):
            half = mixed[kind * HALVED : (kind + 1) * HALVED]
            same = dot(half_ref[0, kind], half[:, :wide])
            other = dot(half_ref[1, kind], half[:, wide:])
            result = None
            for comp in range(3):
                rows = slice(comp * HALVED, (comp + 1) * HALVED)
                term = in_half_block(comp, same[rows] + other[rows, :wide])
                term = term + in_half_block((comp + 1) % 3, other[rows, wide:])
                result = term if result is None else result + term
            results.append(result)
        return unhalve(*results)

    weights = (
        cheb_coef[1] - cheb_coef[3],
        2.0 * (cheb_coef[2] - cheb_coef[4]),
        2.0 * cheb_coef[3],
        2.0 * cheb_coef[4],
    )
    weight = count * scaling
    previous, current, total = None, lattice, None
    for degree in range(4):
        if degree == 1:
            copies[2].wait()
        result = product(current) if degree < 1 else halved_product(current)
        scaled = weights[degree] * result
        total = scaled if total is None else total + scaled
        if degree < 3:
            following = weight * result
            if previous is not None:
                following = 2.0 * following - previous
            previous, current = current, following

    me = lax.axis_index("row") * cols + lax.axis_index("col")
    high, low = split(total)
    held = sites_of(me)
    rows_ref[...] = dot_tn(high, held) + dot_tn(low, held)
    first_weight = cheb_coef[0] - cheb_coef[2] + cheb_coef[4]
    for comp in range(3):
        for vec in range(vecs):
            near = rows_ref[pl.ds(comp * part + vec * units + me, 1), :] * scaling
            out_ref[comp, vec : vec + 1, :] = first_weight * noise_ref[comp, vec : vec + 1, :] + near


def near(packed, noise_field, units, cols, slots):
    vecs = noise_field.shape[1]
    wide = 4 * vecs * units
    tables = kernel_tables()
    vmem = pl.BlockSpec(memory_space=pltpu.VMEM)
    hbm = pl.BlockSpec(memory_space=pltpu.HBM)
    sums = [(SITES, wide), (wide, 3 * wide)] if units > 16 else []
    return pl.pallas_call(
        functools.partial(near_kernel, units, cols, slots, vecs),
        out_shape=pltpu.VMEM((3, vecs, TB), F32),
        in_specs=[vmem] * 2 + [hbm] * 3,
        out_specs=vmem,
        scratch_shapes=[pltpu.VMEM(table.shape, BF16) for table in tables]
        + [pltpu.VMEM((wide, TB), F32), pltpu.SemaphoreType.DMA((3,))]
        + [pltpu.VMEM(shape, F32) for shape in sums],
        compiler_params=pltpu.CompilerParams(vmem_limit_bytes=NEAR_BYTES),
        cost_estimate=pl.CostEstimate(
            flops=4 * 2 * 9 * SITES * SITES * 256, bytes_accessed=8 * 10**6, transcendentals=0
        ),
        name="near_field",
    )(packed, noise_field, *in_hbm(tables))


def per_device(noise_field, offsets, tile_list, send_cells, bead_slot, spectral):
    rows, cols = lax.axis_size("row"), lax.axis_size("col")
    units = rows * cols

    def exchange(blocks, axes=UNIT_AXES):
        return lax.all_to_all(blocks, axes, split_axis=0, concat_axis=0, tiled=True)

    packed = exchange(
        pack(noise_field, offsets, tile_list, send_cells, bead_slot, units, cols)
    )
    field, waves = spectrum(spectral)
    far = sample(packed, field, waves, spectral.shape, send_cells.shape, rows, cols)
    partial = exchange(far, UNIT_AXES[::-1] if units == 16 else UNIT_AXES)
    near_field = near(packed, noise_field, units, cols, tile_list.shape[3])
    return near_field + jnp.sum(partial, axis=0)


def solution(mesh):
    return jax.shard_map(
        per_device,
        mesh=mesh,
        in_specs=(
            P(None, None, ("groups", "row", "col")),
            P(None, ("groups", "row", "col")),
            P(("groups", "row"), "col", None, None),
            P(("groups", "row"), "col", None, None),
            P(("groups", "row", "col")),
            P(None, None, None, ("groups", "row"), "col", None),
        ),
        out_specs=P(None, None, ("groups", "row", "col")),
        check_vma=False,
    )
```
